128 devices in a mesh: wide: 32 (over y, x, core), quad: 4 (over z).
Axes of the slice: x: 4, y: 4, z: 4, core: 2. Of those that a mesh axis runs over, the one named last changes fastest.
Arguments:
- basis: float32 [16, 8388608], P(None, ('wide', 'quad')), may hold values from -6 to 6
- target: float32 [8388608], P(('wide', 'quad')), may hold values from -6 to 6
- sign_bits: int32 [8388608], P(('wide', 'quad')), may hold values from 0 to 1
- samples: int32 [32768], replicated, may hold values from 0 to 8388607
- owners: int32 [32768], replicated, may hold values from 0 to 7
Outputs:
- sketch: float32 [32768, 17], P(('wide', 'quad'))
- gram: float32 [8, 16, 17], P('quad')
The draws below stay inside these ranges and needn't reach their ends.
Inputs may be any that keep to these rules, and one draw needn't show every extreme that they name: `samples`: sampled scenarios may repeat.
All inputs are finite; a program needn't handle non-finite values.
Results may differ from the reference program's by a relative error of at most 0.0003.
Values sent between devices are 32-bit elements; how exact they have to be, the bound alone decides.
No kernel may reach another device: no remote copies, remote signals or barrier semaphores. Data moves between devices by JAX's collectives and lax.ppermute only.
A program may use at most 128 MiB of HBM per device.

```python
import math
import jax
import jax.numpy as jnp
import numpy as np
from jax import lax

COLS = 16
ROWS_DEV = 65536
SCEN = 8388608
SAMPLES = 32768
GROUPS = 8
N_WIDE = 32
N_QUAD = 4


def plant(entries, rng, smallest, largest):
    shape = entries.shape
    index_at = [jax.random.randint(jax.random.fold_in(rng, axis), (), 0, shape[axis]) for axis in range(len(shape))]
    entries = entries.at[tuple(index_at)].set(smallest)
    longest = shape.index(max(shape))
    index_at[longest] = (index_at[longest] + 1) % shape[longest]
    return entries.at[tuple(index_at)].set(largest)


def level_of(own_key, shape, cuts, least, high):
    loudness = 1.0
    for axis_at, shards_of in cuts:
        draws = jax.random.uniform(jax.random.fold_in(jax.random.fold_in(own_key, 6), axis_at), (shards_of,), jnp.float32, least / len(cuts), high / len(cuts))
        loudness = loudness * jnp.repeat(jnp.exp(draws), shape[axis_at] // shards_of).reshape((-1,) + (1,) * (len(shape) - 1 - axis_at))
    return loudness


def rank_table(number_of, lean):
    portions = [(1 << 20) // math.isqrt(standing ** lean) + 1 for standing in range(1, number_of + 1)]
    deviation = 1 + sum(portions) // (1 << 30)
    return np.cumsum(np.array([max(1, weight // deviation) for weight in portions]))


def ranked(rng, shape, count, slope):
    table = rank_table(count, slope)
    pick = jax.random.randint(jax.random.fold_in(rng, 1), shape, 0, int(table[count - 1]))
    rank = jnp.searchsorted(jnp.asarray(table, jnp.int32), pick, side="right")
    return jax.random.permutation(jax.random.fold_in(rng, 2), count)[rank].astype(jnp.int32)


def bell_draw(key, shape, scale, reach, cuts=(), kind=jnp.bfloat16):
    drawn = scale * jax.random.normal(key, shape, jnp.float32)
    if cuts:
        drawn = drawn * level_of(key, shape, cuts, -0.22, 0.18)
    return jnp.clip(drawn, -reach, reach).astype(kind)


def setup_inputs(seed: int = 0) -> dict:
    seeds = jax.random.split(jax.random.key(seed), 6)
    return {
        "basis": bell_draw(seeds[0], (COLS, SCEN), 1.0, 6.0, ((1, 128),), jnp.float32),
        "target": bell_draw(seeds[1], (SCEN,), 1.0, 6.0, ((0, 128),), jnp.float32),
        "sign_bits": plant(jax.random.randint(seeds[2], (SCEN,), 0, 2), jax.random.fold_in(seeds[2], 1), 0, 1).astype(jnp.int32),
        "samples": plant(jax.random.randint(seeds[3], (SAMPLES,), 0, SCEN), jax.random.fold_in(seeds[3], 1), 0, SCEN - 1).astype(jnp.int32),
        "owners": plant(ranked(seeds[4], (SAMPLES,), GROUPS, 2), jax.random.fold_in(seeds[4], 3), 0, GROUPS - 1).astype(jnp.int32),
    }


def butterfly(field):
    width, length = field.shape
    half = 1
    while half < length:
        split = field.reshape(width, length // (2 * half), 2, half)
        upper = split[:, :, 0, :]
        lower = split[:, :, 1, :]
        field = jnp.stack([upper + lower, upper - lower], axis=2).reshape(width, length)
        half = half * 2
    return field


def parity_sign(first, second, nbits):
    count = jnp.zeros_like(first)
    for bit in range(nbits):
        count = count + ((first & second) >> bit) & 1
    return (1 - 2 * (count & 1)).astype(jnp.float32)


def reference(basis, target, sign_bits, samples, owners):
    devices = N_WIDE * N_QUAD
    rows = ROWS_DEV
    nbits = devices.bit_length() - 1
    dev_of = (samples // rows).astype(jnp.int32)
    pos_of = (samples % rows).astype(jnp.int32)
    scale = 1.0 / float(SCEN) ** 0.5

    def step(carry, dev):
        start = (dev * rows).astype(jnp.int32)
        part_basis = lax.dynamic_slice_in_dim(basis, start, rows, 1)
        part_target = lax.dynamic_slice_in_dim(target, start, rows, 0)
        part_bits = lax.dynamic_slice_in_dim(sign_bits, start, rows, 0)
        flip = (1 - 2 * part_bits).astype(jnp.float32)
        signed = jnp.concatenate([part_basis, part_target[None, :]], axis=0) * flip[None, :]
        local = butterfly(signed)
        values = jnp.take(local, pos_of, axis=1)
        sign = parity_sign(dev_of, jnp.full_like(dev_of, dev), nbits)
        return carry + values * sign[None, :], None

    init = jnp.zeros((COLS + 1, SAMPLES), jnp.float32)
    total, _ = lax.scan(step, init, jnp.arange(devices, dtype=jnp.int32))
    sketch = (total * scale).T
    onehot = (owners[:, None] == jnp.arange(GROUPS, dtype=jnp.int32)[None, :]).astype(jnp.float32)
    gram = jnp.einsum("rg,ri,rj->gij", onehot, sketch[:, :COLS], sketch, precision=lax.Precision.HIGHEST)
    gram = gram * (GROUPS / SAMPLES)
    return sketch, gram
```

```python
import math

import jax
import jax.numpy as jnp
from jax import lax
from jax.experimental import pallas as pl
from jax.experimental.pallas import tpu as pltpu
from jax.sharding import PartitionSpec as P

GROUPS = 8
AXES = ("wide", "quad")
LANES = 128
COLS = 17
PAD = 24
SIDE = 256
ORDERS = (("y", "x", "z"), ("z", "y", "x"))
PEEL = 6
STEP = 4


def number(y, x, c, z):
    return ((y * 4 + x) * 2 + c) * 4 + z


def shift(axis, off):
    pairs = []
    for y in range(4):
        for x in range(4):
            for c in range(2):
                for z in range(4):
                    at = {"y": y, "x": x, "c": c, "z": z}
                    size = 2 if axis == "c" else 4
                    to = dict(at)
                    to[axis] = (at[axis] + off) % size
                    pairs.append((number(**at), number(**to)))
    return pairs


def fold(v):
    v = v ^ (v >> 8)
    v = v ^ (v >> 4)
    v = v ^ (v >> 2)
    v = v ^ (v >> 1)
    return v & 1


def lane_take(tile, index):
    return jnp.take_along_axis(tile, index, axis=1)


def sort_kernel(pos_ref, samples_ref, keys_ref, ends_ref, scratch):
    me = pos_ref[0]
    sub = lax.broadcasted_iota(jnp.int32, (8, LANES), 0)
    lane = lax.broadcasted_iota(jnp.int32, (8, LANES), 1)
    for c in range(2):
        v = []
        for i in range(16):
            s = samples_ref[i, c]
            p = s & 65535
            place = (((p >> 7) & 1) << 15) | ((p >> 8) << 7) | (p & 127)
            odd = fold((s >> 16) & me)
            r = i * 1024 + sub * LANES + lane
            v.append((place << 15) | (r << 1) | odd)
        for k in range(1, 15):
            for b in (k - 1, k):
                if b == 0 or b == 14:
                    continue
                if b < 4:
                    v = [~t if (i >> b) & 1 else t for i, t in enumerate(v)]
                else:
                    bit = (sub >> (b - 4)) if b < 7 else (lane >> (b - 7))
                    m = -(bit & 1)
                    v = [t ^ m for t in v]
            for j in range(k - 1, -1, -1):
                if j < 4:
                    new = list(v)
                    for i in range(16):
                        if not (i >> j) & 1:
                            a, b = v[i], v[i | (1 << j)]
                            new[i] = jnp.minimum(a, b)
                            new[i | (1 << j)] = jnp.maximum(a, b)
                    v = new
                elif j < 7:
                    d = 1 << (j - 4)
                    up = (sub & d) != 0
                    new = []
                    for t in v:
                        prev = pltpu.roll(t, d, 0)
                        nxt = prev if d == 4 else pltpu.roll(t, 8 - d, 0)
                        new.append(jnp.where(up, jnp.maximum(t, prev), jnp.minimum(t, nxt)))
                    v = new
                else:
                    d = 1 << (j - 7)
                    up = (lane & d) != 0
                    other = lane ^ d
                    new = []
                    for t in v:
                        o = lane_take(t, other)
                        new.append(jnp.where(up, jnp.maximum(t, o), jnp.minimum(t, o)))
                    v = new
        for i in range(16):
            scratch[pl.ds(i, 8, stride=16), :] = v[i]
        ends_ref[2 * c : 2 * c + 1, :] = scratch[0:1, :] >> 22
        ends_ref[2 * c + 1 : 2 * c + 2, :] = scratch[127:128, :] >> 22
        keys_ref[c * LANES : (c + 1) * LANES, :] = scratch[...].T


def sort_call(pos, samples):
    return pl.pallas_call(
        sort_kernel,
        out_shape=(
            jax.ShapeDtypeStruct((256, LANES), jnp.int32),
            jax.ShapeDtypeStruct((4, LANES), jnp.int32),
        ),
        in_specs=[pl.BlockSpec(memory_space=pltpu.SMEM), pl.BlockSpec(memory_space=pltpu.VMEM)],
        out_specs=(pl.BlockSpec(memory_space=pltpu.VMEM),) * 2,
        scratch_shapes=[pltpu.VMEM((LANES, LANES), jnp.int32)],
        name="sort_slots",
    )(pos, samples)


def split(x):
    hi = x.astype(jnp.bfloat16)
    lo = (x - hi.astype(jnp.float32)).astype(jnp.bfloat16)
    return hi, lo


def table256():
    a = lax.broadcasted_iota(jnp.int32, (SIDE, SIDE), 0)
    b = lax.broadcasted_iota(jnp.int32, (SIDE, SIDE), 1)
    return (1 - 2 * fold(a & b)).astype(jnp.float32).astype(jnp.bfloat16)


def dot(a, b):
    return lax.dot_general(a, b, (((1,), (0,)), ((), ())), preferred_element_type=jnp.float32)


def mix_kernel(scale, pos_ref, ends_ref, basis_ref, target_ref, bits_ref, keys_ref, k0, s0, k1, s1, tab):
    walsh = table256()
    flips = [(1 - 2 * bits_ref[pl.ds(bh, SIDE, stride=2), :]).astype(jnp.float32) for bh in range(2)]
    flip = jnp.concatenate(flips, axis=1)
    for k in range(COLS):
        if k < 16:
            base = (k // 8) * 4096 + k % 8
            halves = [basis_ref[pl.ds(base + 8 * bh, SIDE, stride=16), :] for bh in range(2)]
        else:
            halves = [target_ref[pl.ds(bh, SIDE, stride=2), :] for bh in range(2)]
        x = jnp.concatenate(halves, axis=1) * flip
        hi, lo = split(x)
        y = dot(hi, walsh) + dot(lo, walsh)
        hi, lo = split(y)
        z = dot(walsh, hi) + dot(walsh, lo)
        for bh in range(2):
            tab[pl.ds(bh * SIDE * PAD + k, SIDE, stride=PAD), :] = z[:, bh * LANES : (bh + 1) * LANES]

    core = pos_ref[1]
    for b, outs in ((0, (k0, s0)), (1, (k1, s1))):
        m1, m2, m3 = (pos_ref[2 + "yxz".index(a)] for a in ORDERS[b])
        for rel_core, out in enumerate(outs):
            c = core ^ rel_core

            def group(it, _, b=b, c=c, out=out, m1=m1, m2=m2, m3=m3):
                s12 = (((it >> 2) + m1) & 3) * 4 + (((it & 3) + m2) & 3)
                lows, spans, lanes_of, rows_of, weights = [], [], [], [], []
                for r3 in range(4):
                    j = b * 64 + s12 * 4 + ((r3 + m3) & 3)
                    key = jnp.broadcast_to(keys_ref[pl.ds(c * LANES + j, 1), :], (8, LANES))
                    low = ends_ref[2 * c, j]
                    lows.append(low)
                    spans.append(ends_ref[2 * c + 1, j] - low + 1)
                    lanes_of.append((key >> 15) & 127)
                    rows_of.append((key >> 22) - low)
                    weights.append(jnp.where((key & 1) != 0, -scale, scale))
                most = jnp.maximum(jnp.maximum(spans[0], spans[1]), jnp.maximum(spans[2], spans[3]))

                def add_rows(first, count, acc):
                    acc = list(acc)
                    for u in range(count):
                        for q in range(4):
                            row = jnp.minimum(lows[q] + first + u, 511)
                            hit = rows_of[q] == first + u
                            for t in range(3):
                                tile = tab[pl.ds(pl.multiple_of(row * PAD + 8 * t, 8), 8), :]
                                acc[q * 3 + t] = jnp.where(hit, lane_take(tile, lanes_of[q]), acc[q * 3 + t])
                    return tuple(acc)

                acc = tuple(jnp.zeros((8, LANES), jnp.float32) for _ in range(12))
                acc = add_rows(0, PEEL, acc)
                more = (jnp.maximum(most - PEEL, 0) + STEP - 1) // STEP
                acc = lax.fori_loop(0, more, lambda n, a: add_rows(PEEL + n * STEP, STEP, a), acc)
                base = it * (4 * COLS)
                for r3 in range(4):
                    for t in range(2):
                        out[pl.ds(base + r3 + 32 * t, 8, stride=4), :] = acc[r3 * 3 + t] * weights[r3]
                    out[pl.ds(base + r3 + 64, 1), :] = acc[r3 * 3 + 2][0:1] * weights[r3][0:1]
                return 0

            lax.fori_loop(0, 16, group, 0)


def mix_call(scale, pos, ends, basis, target, bits, keys):
    vmem = pl.BlockSpec(memory_space=pltpu.VMEM)
    smem = pl.BlockSpec(memory_space=pltpu.SMEM)
    part = jax.ShapeDtypeStruct((16 * 4 * COLS, LANES), jnp.float32)
    return pl.pallas_call(
        lambda *refs: mix_kernel(scale, *refs),
        out_shape=(part,) * 4,
        in_specs=[smem, smem, vmem, vmem, vmem, vmem],
        out_specs=(vmem,) * 4,
        scratch_shapes=[pltpu.VMEM((512 * PAD, LANES), jnp.float32)],
        compiler_params=pltpu.CompilerParams(vmem_limit_bytes=48 * 2**20),
        name="mix_and_pick",
    )(pos, ends, basis, target, bits, keys)


def own_block(pos_ref, b):
    m1, m2, m3 = (pos_ref[2 + "yxz".index(a)] for a in ORDERS[b])
    return b * 64 + (m1 * 4 + m2) * 4 + m3


def gram_kernel(factor, pos_ref, v0_ref, v1_ref, keys_ref, owners_ref, o0, o1, o2, o3):
    core, quad = pos_ref[1], pos_ref[4]
    sub = lax.broadcasted_iota(jnp.int32, (8, LANES), 0)
    values = jnp.concatenate([v0_ref[...], v1_ref[...]], axis=1)
    owner = []
    for b in range(2):
        row = core * LANES + own_block(pos_ref, b)
        r = (jnp.broadcast_to(keys_ref[pl.ds(row, 1), :], (8, LANES)) >> 1) & 16383
        found = jnp.zeros((8, LANES), jnp.int32)
        for i in range(16):
            tile = owners_ref[i, core]
            found = jnp.where((r >> 10) == i, lane_take(tile, r & 127), found)
        found = jnp.where(((r >> 7) & 7) == sub, found, 0)
        owner.append(jnp.sum(found, axis=0, keepdims=True))
    owner = jnp.concatenate(owner, axis=1)
    for rel, out in enumerate((o0, o1, o2, o3)):
        first = 2 * ((rel + quad) & 3)
        left = jnp.concatenate(
            [jnp.where(owner == first + g, values[:16], 0.0) for g in range(2)], axis=0
        )
        out[...] = factor * lax.dot_general(
            left, values, (((1,), (1,)), ((), ())),
            precision=lax.Precision.HIGHEST, preferred_element_type=jnp.float32,
        )


def gram_call(factor, pos, v0, v1, keys, owners):
    vmem = pl.BlockSpec(memory_space=pltpu.VMEM)
    smem = pl.BlockSpec(memory_space=pltpu.SMEM)
    return pl.pallas_call(
        lambda *refs: gram_kernel(factor, *refs),
        out_shape=(jax.ShapeDtypeStruct((32, COLS), jnp.float32),) * 4,
        in_specs=[smem] + [vmem] * 4,
        out_specs=(vmem,) * 4,
        name="slot_gram",
    )(pos, v0, v1, keys, owners)


def rank_kernel(pos_ref, keys_ref, rank_ref, acc):
    core = pos_ref[1]
    first = ((pos_ref[2] * 4 + pos_ref[3]) * 4 + pos_ref[4]) * 256
    sub = lax.broadcasted_iota(jnp.int32, (SIDE, LANES), 0)
    lane = lax.broadcasted_iota(jnp.int32, (1, LANES), 1)
    acc[...] = jnp.zeros_like(acc)

    def step(n, _):
        total = acc[...]
        for u in range(8):
            j = n * 8 + u
            r = ((keys_ref[pl.ds(core * LANES + j, 1), :] >> 1) & 16383) - first
            slot = j * LANES + lane
            total = jnp.where(sub == r, slot, total)
        acc[...] = total
        return 0

    lax.fori_loop(0, LANES // 8, step, 0)
    ones = jnp.ones((8, LANES), jnp.float32)
    rank_ref[...] = lax.dot_general(
        ones, acc[...].astype(jnp.float32), (((1,), (1,)), ((), ())),
        precision=lax.Precision.HIGHEST, preferred_element_type=jnp.float32,
    ).astype(jnp.int32)


def rank_call(pos, keys):
    vmem = pl.BlockSpec(memory_space=pltpu.VMEM)
    smem = pl.BlockSpec(memory_space=pltpu.SMEM)
    return pl.pallas_call(
        rank_kernel,
        out_shape=jax.ShapeDtypeStruct((8, SIDE), jnp.int32),
        in_specs=[smem, vmem],
        out_specs=vmem,
        scratch_shapes=[pltpu.VMEM((SIDE, LANES), jnp.int32)],
        name="row_rank",
    )(pos, keys)


def pick_kernel(pos_ref, rank_ref, *refs):
    parts, out = refs[:8], refs[8]
    rows = 16 * COLS
    at = lax.broadcasted_iota(jnp.int32, (rows, LANES), 0)
    code_row = (at // (4 * COLS)) * 4 + (at & 3)
    er = lax.broadcasted_iota(jnp.int32, (rows, COLS), 0)
    ek = lax.broadcasted_iota(jnp.int32, (rows, COLS), 1)
    collect = jnp.where((er % (4 * COLS)) // 4 == ek, 1.0, 0.0)
    for h in range(2):
        slot = rank_ref[:, h * LANES : (h + 1) * LANES]
        block = slot >> 7
        b = block >> 6
        rel = []
        for n in range(3):
            mine = [pos_ref[2 + "yxz".index(ORDERS[q][n])] for q in range(2)]
            mine = jnp.where(b == 0, mine[0], mine[1])
            rel.append((((block >> (4 - 2 * n)) & 3) - mine) & 3)
        index = slot & 127
        first = b * 4 + rel[0]
        acc = [jnp.zeros((8, LANES), jnp.float32)] * (rows // 8)
        for n, part in enumerate(parts):
            hit = first == n
            for t in range(rows // 8):
                acc[t] = jnp.where(hit, lane_take(part[8 * t : 8 * t + 8, :], index), acc[t])
        code = (rel[1] * 4 + rel[2])[0:1]
        chosen = jnp.where(code_row == code, jnp.concatenate(acc, axis=0), 0.0)
        out[h * LANES : (h + 1) * LANES, :] = lax.dot_general(
            chosen, collect, (((0,), (0,)), ((), ())),
            precision=lax.Precision.HIGHEST, preferred_element_type=jnp.float32,
        )


def pick_call(pos, rank, parts):
    vmem = pl.BlockSpec(memory_space=pltpu.VMEM)
    smem = pl.BlockSpec(memory_space=pltpu.SMEM)
    return pl.pallas_call(
        pick_kernel,
        out_shape=jax.ShapeDtypeStruct((SIDE, COLS), jnp.float32),
        in_specs=[smem] + [vmem] * 9,
        out_specs=vmem,
        name="pick_rows",
    )(pos, rank, *parts)


def send(v, axis, off):
    return lax.ppermute(v, AXES, shift(axis, off))


def shards(basis, target, sign_bits, samples, owners):
    rows = basis.shape[1]
    total_samples = samples.shape[0]
    scale = 1.0 / math.sqrt(rows * 128)
    wide = lax.axis_index("wide")
    z = lax.axis_index("quad")
    core, x, y = wide & 1, (wide >> 1) & 3, wide >> 3
    pos = jnp.stack([wide * 4 + z, core, y, x, z, z, z, z]).astype(jnp.int32)

    keys, ends = sort_call(pos, samples.reshape(16, 2, 8, LANES))
    tiles = basis.reshape(2, 8, 512, LANES).transpose(0, 2, 1, 3).reshape(8192, LANES)
    k0, s0, k1, s1 = mix_call(
        scale, pos, ends, tiles, target.reshape(512, LANES), sign_bits.reshape(512, LANES), keys
    )
    rank = rank_call(pos, keys)
    vals = [k0 + send(s0, "c", 1), k1 + send(s1, "c", 1)]
    for n in range(2):
        got = []
        for b in range(2):
            quarter = vals[b].reshape(4, -1, LANES)
            got.append([quarter[0]] + [send(quarter[o], ORDERS[b][n], o) for o in (2, 1, 3)])
        vals = [(g[0] + g[1]) + (g[2] + g[3]) for g in got]
    got = []
    for b in range(2):
        quarter = vals[b].reshape(COLS, 4, LANES)
        got.append([quarter[:, 0]] + [send(quarter[:, o], ORDERS[b][2], o) for o in (2, 1, 3)])
    vals = [(g[0] + g[1]) + (g[2] + g[3]) for g in got]

    grams = gram_call(GROUPS / total_samples, pos, vals[0], vals[1], keys, owners.reshape(16, 2, 8, LANES))
    gram = sum([send(grams[o], "z", o) for o in (1, 2, 3)], grams[0])
    for axis in ("y", "x"):
        gram = sum([send(gram, axis, o) for o in (1, 2, 3)], gram)
    gram = gram + send(gram, "c", 1)

    full = []
    for b in range(2):
        own = vals[b]
        axis = ORDERS[b][2]
        own = jnp.stack([own] + [send(own, axis, -o) for o in (1, 2, 3)], axis=1).reshape(4 * COLS, LANES)
        axis = ORDERS[b][1]
        own = jnp.concatenate([own] + [send(own, axis, -o) for o in (1, 2, 3)], axis=0)
        axis = ORDERS[b][0]
        full += [own] + [send(own, axis, -o) for o in (1, 2, 3)]
    sketch = pick_call(pos, rank, full)
    return sketch, gram.reshape(2, 16, COLS)


def solution(mesh):
    placed = (P(None, AXES), P(AXES), P(AXES), P(), P())
    return jax.shard_map(
        shards,
        mesh=mesh,
        in_specs=placed,
        out_specs=(P(AXES, None), P("quad", None, None)),
        check_vma=False,
    )
```

```python
import math

import jax
import jax.numpy as jnp
from jax import lax
from jax.experimental import pallas as pl
from jax.experimental.pallas import tpu as pltpu
from jax.sharding import PartitionSpec as P

GROUPS = 8
AXES = ("wide", "quad")
LANES = 128
COLS = 17
SIDE = 256
PEEL = 20
STEP = 4


def number(y, x, c, z):
    return ((y * 4 + x) * 2 + c) * 4 + z


def shift(axis, off):
    pairs = []
    for y in range(4):
        for x in range(4):
            for c in range(2):
                for z in range(4):
                    at = {"y": y, "x": x, "c": c, "z": z}
                    size = 2 if axis == "c" else 4
                    to = dict(at)
                    to[axis] = (at[axis] + off) % size
                    pairs.append((number(**at), number(**to)))
    return pairs


def fold(v):
    v = v ^ (v >> 8)
    v = v ^ (v >> 4)
    v = v ^ (v >> 2)
    v = v ^ (v >> 1)
    return v & 1


def lane_take(tile, index):
    return jnp.take_along_axis(tile, index, axis=1)


def bitonic(v, sub, lane):
    for k in range(1, 13):
        for b in (k - 1, k):
            if b == 0 or b == 12:
                continue
            if b < 4:
                v = [~t if (i >> b) & 1 else t for i, t in enumerate(v)]
            else:
                bit = (sub >> (b - 4)) if b < 7 else (lane >> (b - 7))
                m = -(bit & 1)
                v = [t ^ m for t in v]
        for j in range(k - 1, -1, -1):
            if j < 4:
                new = list(v)
                for i in range(16):
                    if not (i >> j) & 1:
                        a, b = v[i], v[i | (1 << j)]
                        new[i] = jnp.minimum(a, b)
                        new[i | (1 << j)] = jnp.maximum(a, b)
                v = new
            elif j < 7:
                d = 1 << (j - 4)
                up = (sub & d) != 0
                new = []
                for t in v:
                    prev = pltpu.roll(t, d, 0)
                    nxt = prev if d == 4 else pltpu.roll(t, 8 - d, 0)
                    new.append(jnp.where(up, jnp.maximum(t, prev), jnp.minimum(t, nxt)))
                v = new
            else:
                d = 1 << (j - 7)
                up = (lane & d) != 0
                other = lane ^ d
                new = []
                for t in v:
                    o = lane_take(t, other)
                    new.append(jnp.where(up, jnp.maximum(t, o), jnp.minimum(t, o)))
                v = new
    return v


def sort_kernel(pos_ref, samples_ref, keys_ref, ends_ref, rank_ref, scratch):
    me, core = pos_ref[0], pos_ref[1]
    sub = lax.broadcasted_iota(jnp.int32, (8, LANES), 0)
    lane = lax.broadcasted_iota(jnp.int32, (8, LANES), 1)
    both = []
    for c in range(2):
        v = []
        for i in range(16):
            s = samples_ref[i, c]
            p = s & 65535
            place = (((p >> 7) & 1) << 15) | ((p >> 8) << 7) | (p & 127)
            odd = fold((s >> 16) & me)
            r = i * 256 + sub * 32 + (lane & 31)
            v.append((place << 13) | (r << 1) | odd)
        v = bitonic(v, sub, lane)
        both.append(v)
        for i in range(16):
            scratch[pl.ds(i, 8, stride=16), :] = v[i]
        ends_ref[2 * c : 2 * c + 1, :] = scratch[0:1, :] >> 20
        ends_ref[2 * c + 1 : 2 * c + 2, :] = scratch[127:128, :] >> 20
        keys_ref[c * LANES : (c + 1) * LANES, :] = scratch[...].T
    v = []
    for i in range(16):
        key = jnp.where(core == 0, both[0][i], both[1][i])
        slot = (lane & 31) * LANES + sub * 16 + i
        v.append((((key >> 1) & 4095) << 12) | slot)
    v = bitonic(v, sub, lane)
    for i in range(16):
        scratch[pl.ds(i, 8, stride=16), :] = v[i] & 4095
    rank_ref[...] = scratch[...].T


VMEM = pl.BlockSpec(memory_space=pltpu.VMEM)
SMEM = pl.BlockSpec(memory_space=pltpu.SMEM)


def sort_call(pos, samples):
    return pl.pallas_call(
        sort_kernel,
        out_shape=(
            jax.ShapeDtypeStruct((256, LANES), jnp.int32),
            jax.ShapeDtypeStruct((4, LANES), jnp.int32),
            jax.ShapeDtypeStruct((LANES, LANES), jnp.int32),
        ),
        in_specs=[SMEM, VMEM],
        out_specs=(VMEM,) * 3,
        scratch_shapes=[pltpu.VMEM((LANES, LANES), jnp.int32)],
        compiler_params=pltpu.CompilerParams(vmem_limit_bytes=8 * 2**20),
        cost_estimate=pl.CostEstimate(flops=20_000_000, bytes_accessed=20_000_000, transcendentals=0),
        name="sort_slots",
    )(pos, samples)


def split(x):
    hi = x.astype(jnp.bfloat16)
    lo = (x - hi.astype(jnp.float32)).astype(jnp.bfloat16)
    return hi, lo


def dot(a, b):
    return lax.dot_general(a, b, (((1,), (0,)), ((), ())), preferred_element_type=jnp.float32)


def mix_kernel(basis_ref, target_ref, bits_ref, tab, last):
    a = lax.broadcasted_iota(jnp.int32, (SIDE, SIDE), 0)
    b = lax.broadcasted_iota(jnp.int32, (SIDE, SIDE), 1)
    walsh = (1 - 2 * fold(a & b)).astype(jnp.float32).astype(jnp.bfloat16)
    flips = [(1 - 2 * bits_ref[pl.ds(bh, SIDE, stride=2), :]).astype(jnp.float32) for bh in range(2)]
    flip = jnp.concatenate(flips, axis=1)
    for k in range(COLS):
        if k < 16:
            base = (k // 8) * 4096 + k % 8
            halves = [basis_ref[pl.ds(base + 8 * bh, SIDE, stride=16), :] for bh in range(2)]
        else:
            halves = [target_ref[pl.ds(bh, SIDE, stride=2), :] for bh in range(2)]
        x = jnp.concatenate(halves, axis=1) * flip
        hi, lo = split(x)
        y = dot(hi, walsh) + dot(lo, walsh)
        hi, lo = split(y)
        z = dot(walsh, hi) + dot(walsh, lo)
        for bh in range(2):
            half = z[:, bh * LANES : (bh + 1) * LANES]
            if k < 16:
                tab[pl.ds(bh * SIDE * 16 + k, SIDE, stride=16), :] = half
            else:
                last[bh * SIDE : (bh + 1) * SIDE, :] = half


def mix_call(basis, target, bits):
    return pl.pallas_call(
        mix_kernel,
        out_shape=(
            jax.ShapeDtypeStruct((512 * 16, LANES), jnp.float32),
            jax.ShapeDtypeStruct((512, LANES), jnp.float32),
        ),
        in_specs=[VMEM] * 3,
        out_specs=(VMEM,) * 2,
        compiler_params=pltpu.CompilerParams(vmem_limit_bytes=16 * 2**20),
        cost_estimate=pl.CostEstimate(flops=2 * 2**31, bytes_accessed=20_000_000, transcendentals=0),
        name="local_walsh",
    )(basis, target, bits)


def slots_kernel(scale, off, pos_ref, ends_ref, tab, last, keys_ref, keep, give):
    core = pos_ref[1]
    z = (pos_ref[4] + off) & 3
    sub = lax.broadcasted_iota(jnp.int32, (8, LANES), 0)
    for rel_core, out in enumerate((keep, give)):
        c = core ^ rel_core

        def group(it, _, c=c, out=out):
            lows, tiles, lanes_of, rows_of, subrows, weights = [], [], [], [], [], []
            most, many = jnp.int32(0), jnp.int32(0)
            for q in range(4):
                j = z * 32 + it * 4 + q
                key = jnp.broadcast_to(keys_ref[pl.ds(c * LANES + j, 1), :], (8, LANES))
                low, high = ends_ref[2 * c, j], ends_ref[2 * c + 1, j]
                lows.append(low)
                tiles.append(low >> 3)
                most = jnp.maximum(most, high - low + 1)
                many = jnp.maximum(many, (high >> 3) - (low >> 3) + 1)
                lanes_of.append((key >> 13) & 127)
                rows_of.append((key >> 20) - low)
                subrows.append((key >> 20) - (low >> 3) * 8 - sub)
                weights.append(jnp.where((key & 1) != 0, -scale, scale))

            def add_rows(first, count, acc):
                acc = list(acc)
                for u in range(count):
                    for q in range(4):
                        row = jnp.minimum(lows[q] + first + u, 511)
                        hit = rows_of[q] == first + u
                        for t in range(2):
                            tile = tab[pl.ds(pl.multiple_of(row * 16 + 8 * t, 8), 8), :]
                            acc[q * 2 + t] = jnp.where(hit, lane_take(tile, lanes_of[q]), acc[q * 2 + t])
                return tuple(acc)

            def add_last(first, count, acc):
                acc = list(acc)
                for u in range(count):
                    for q in range(4):
                        row = jnp.minimum(tiles[q] + first + u, 63)
                        tile = last[pl.ds(pl.multiple_of(row * 8, 8), 8), :]
                        hit = subrows[q] == (first + u) * 8
                        acc[q] = jnp.where(hit, lane_take(tile, lanes_of[q]), acc[q])
                return tuple(acc)

            zero = jnp.zeros((8, LANES), jnp.float32)
            acc = add_rows(0, PEEL, (zero,) * 8)
            more = (jnp.maximum(most - PEEL, 0) + STEP - 1) // STEP
            acc = lax.fori_loop(0, more, lambda n, a: add_rows(PEEL + n * STEP, STEP, a), acc)
            tail = add_last(0, 4, (zero,) * 4)
            tail = lax.fori_loop(4, jnp.maximum(many, 4), lambda n, a: add_last(n, 1, a), tail)
            base = it * (4 * COLS)
            for q in range(4):
                for t in range(2):
                    out[pl.ds(base + q + 32 * t, 8, stride=4), :] = acc[q * 2 + t] * weights[q]
                line = jnp.sum(tail[q], axis=0, keepdims=True)
                out[pl.ds(base + q + 64, 1), :] = line * weights[q][0:1]
            return 0

        lax.fori_loop(0, 8, group, 0)


def slots_call(scale, off, pos, ends, tab, last, keys):
    part = jax.ShapeDtypeStruct((8 * 4 * COLS, LANES), jnp.float32)
    return pl.pallas_call(
        lambda *refs: slots_kernel(scale, off, *refs),
        out_shape=(part,) * 2,
        in_specs=[SMEM, SMEM, VMEM, VMEM, VMEM],
        out_specs=(VMEM,) * 2,
        compiler_params=pltpu.CompilerParams(vmem_limit_bytes=12 * 2**20),
        cost_estimate=pl.CostEstimate(flops=20_000_000, bytes_accessed=22_000_000, transcendentals=0),
        name=f"take_slots_{off}",
    )(pos, ends, tab, last, keys)


def order_kernel(pos_ref, rank_ref, *refs):
    parts, outs, table = refs[:4], refs[4:8], refs[8]
    y, z = pos_ref[2], pos_ref[4]
    table[...] = (parts[0][...] + parts[1][...]) + (parts[2][...] + parts[3][...])
    rows = 8 * COLS
    at = lax.broadcasted_iota(jnp.int32, (rows, LANES), 0)
    code = (at // (4 * COLS)) * 4 + (at & 3)
    ck = lax.broadcasted_iota(jnp.int32, (24, rows), 0)
    cr = lax.broadcasted_iota(jnp.int32, (24, rows), 1)
    collect = jnp.where((cr % (4 * COLS)) // 4 == ck, 1.0, 0.0).astype(jnp.bfloat16)

    def step(i, _):
        for rel, out in enumerate(outs):
            line = z * 32 + ((y + rel) & 3) * 8 + i
            slot = jnp.broadcast_to(rank_ref[pl.ds(line, 1), :], (8, LANES))
            index = slot & 127
            pair = slot >> 10
            acc = [jnp.zeros((8, LANES), jnp.float32)] * COLS
            for n in range(4):
                hit = pair == n
                for t in range(COLS):
                    tile = table[n * rows + 8 * t : n * rows + 8 * t + 8, :]
                    acc[t] = jnp.where(hit, lane_take(tile, index), acc[t])
            chosen = jnp.where(code == ((slot >> 7) & 7)[0:1], jnp.concatenate(acc, axis=0), 0.0)
            hi, lo = split(chosen)
            values = dot(collect, hi) + dot(collect, lo)
            for t in range(2):
                out[pl.ds(i + 64 * t, 8, stride=8), :] = values[8 * t : 8 * t + 8]
            out[pl.ds(i + 128, 1), :] = values[16:17]
        return 0

    lax.fori_loop(0, 8, step, 0)


def order_call(pos, rank, parts):
    rows = 8 * COLS
    return pl.pallas_call(
        order_kernel,
        out_shape=(jax.ShapeDtypeStruct((rows, LANES), jnp.float32),) * 4,
        in_specs=[SMEM] + [VMEM] * 5,
        out_specs=(VMEM,) * 4,
        scratch_shapes=[pltpu.VMEM((4 * rows, LANES), jnp.float32)],
        compiler_params=pltpu.CompilerParams(vmem_limit_bytes=8 * 2**20),
        cost_estimate=pl.CostEstimate(flops=20_000_000, bytes_accessed=18_000_000, transcendentals=0),
        name="given_order",
    )(pos, rank, *parts)


def finish_kernel(factor, pos_ref, owners_ref, p0, p1, p2, p3, sketch, gram, table):
    core, y, x, z = pos_ref[1], pos_ref[2], pos_ref[3], pos_ref[4]
    table[0 : 8 * COLS, :] = (p0[...] + p1[...]) + (p2[...] + p3[...])
    table[8 * COLS :, :] = jnp.zeros((24 * 8 - 8 * COLS, LANES), jnp.float32)
    for h in range(2):
        sketch[:, h * LANES : (h + 1) * LANES] = table[pl.ds(2 * x + h, 24, stride=8), :][:COLS]
    pieces, lefts = [], []
    for tx in range(4):
        for h in range(2):
            v = table[pl.ds(2 * tx + h, 24, stride=8), :]
            owner = owners_ref[y * 4 + tx, core, pl.ds(2 * z + h, 1), :]
            lefts.append(jnp.concatenate([jnp.where(owner == g, v[:16], 0.0) for g in range(GROUPS)], axis=0))
            pieces.append(v)
    value = jnp.concatenate(pieces, axis=1)
    left = jnp.concatenate(lefts, axis=1)
    total = lax.dot_general(
        value, left, (((1,), (1,)), ((), ())),
        precision=lax.Precision.HIGHEST, preferred_element_type=jnp.float32,
    )
    gram[...] = factor * total[:COLS]


def finish_call(factor, pos, owners, parts):
    return pl.pallas_call(
        lambda *refs: finish_kernel(factor, *refs),
        out_shape=(
            jax.ShapeDtypeStruct((COLS, SIDE), jnp.float32),
            jax.ShapeDtypeStruct((COLS, LANES), jnp.float32),
        ),
        in_specs=[SMEM] + [VMEM] * 5,
        out_specs=(VMEM,) * 2,
        scratch_shapes=[pltpu.VMEM((24 * 8, LANES), jnp.float32)],
        compiler_params=pltpu.CompilerParams(vmem_limit_bytes=8 * 2**20),
        name="rows_and_gram",
    )(pos, owners, *parts)


def send(v, axis, off):
    return lax.ppermute(v, AXES, shift(axis, off))


def shards(basis, target, sign_bits, samples, owners):
    rows = basis.shape[1]
    total_samples = samples.shape[0]
    scale = 1.0 / math.sqrt(rows * 128)
    wide = lax.axis_index("wide")
    z = lax.axis_index("quad")
    core, x, y = wide & 1, (wide >> 1) & 3, wide >> 3
    pos = jnp.stack([wide * 4 + z, core, y, x, z, z, z, z]).astype(jnp.int32)

    lined = samples.reshape(16, 2, 4, 8, 32).transpose(0, 1, 3, 2, 4).reshape(16, 2, 8, LANES)
    keys, ends, rank = sort_call(pos, lined)
    tiles = basis.reshape(2, 8, 512, LANES).transpose(0, 2, 1, 3).reshape(8192, LANES)
    tab, last = mix_call(tiles, target.reshape(512, LANES), sign_bits.reshape(512, LANES))
    parts, held = [], []
    for n, off in enumerate((2, 1, 3, 0)):
        if n >= 2:
            keys, held[n - 2] = lax.optimization_barrier((keys, held[n - 2]))
        keep, give = slots_call(scale, off, pos, ends, tab, last, keys)
        held.append(keep + send(give, "c", 1))
        if n >= 2:
            parts.append(send(held[n - 2], "z", (2, 1)[n - 2]))
    parts += [send(held[2], "z", 3), held[3]]
    lines = order_call(pos, rank, parts)
    line = (lines[0] + send(lines[2], "y", 2)) + (send(lines[1], "y", 1) + send(lines[3], "y", 3))
    around = [line] + [send(line, "x", off) for off in (2, 1, 3)]
    sketch, gram = finish_call(GROUPS / total_samples, pos, owners.reshape(16, 2, 8, LANES), around)
    for axis in ("z", "y"):
        gram = (gram + send(gram, axis, 2)) + (send(gram, axis, 1) + send(gram, axis, 3))
    gram = gram + send(gram, "c", 1)
    own = lax.dynamic_slice_in_dim(gram, z * 32, 32, 1)
    return sketch.T, own.T.reshape(2, 16, COLS)


def solution(mesh):
    placed = (P(None, AXES), P(AXES), P(AXES), P(), P())
    return jax.shard_map(
        shards,
        mesh=mesh,
        in_specs=placed,
        out_specs=(P(AXES, None), P("quad", None, None)),
        check_vma=False,
    )
```

```python
import math

import jax
import jax.numpy as jnp
from jax import lax
from jax.experimental import pallas as pl
from jax.experimental.pallas import tpu as pltpu
from jax.sharding import PartitionSpec as P

GROUPS = 8
AXES = ("wide", "quad")
LANES = 128
COLS = 17
SIDE = 256
PEEL = 20
STEP = 4
EIGHTHS = 4
ROWS = 512
ROWS_PAD = 536


def number(y, x, c, z):
    return ((y * 4 + x) * 2 + c) * 4 + z


def shift(axis, off):
    pairs = []
    for y in range(4):
        for x in range(4):
            for c in range(2):
                for z in range(4):
                    at = {"y": y, "x": x, "c": c, "z": z}
                    size = 2 if axis == "c" else 4
                    to = dict(at)
                    to[axis] = (at[axis] + off) % size
                    pairs.append((number(**at), number(**to)))
    return pairs


def fold(v):
    v = v ^ (v >> 8)
    v = v ^ (v >> 4)
    v = v ^ (v >> 2)
    v = v ^ (v >> 1)
    return v & 1


def lane_take(tile, index):
    return jnp.take_along_axis(tile, index, axis=1)


def bitonic(v, sub, lane):
    for k in range(1, 13):
        for b in (k - 1, k):
            if b == 0 or b == 12:
                continue
            if b < 4:
                v = [~t if (i >> b) & 1 else t for i, t in enumerate(v)]
            else:
                bit = (sub >> (b - 4)) if b < 7 else (lane >> (b - 7))
                m = -(bit & 1)
                v = [t ^ m for t in v]
        for j in range(k - 1, -1, -1):
            if j < 4:
                new = list(v)
                for i in range(16):
                    if not (i >> j) & 1:
                        a, b = v[i], v[i | (1 << j)]
                        new[i] = jnp.minimum(a, b)
                        new[i | (1 << j)] = jnp.maximum(a, b)
                v = new
            elif j < 7:
                d = 1 << (j - 4)
                up = (sub & d) != 0
                new = []
                for t in v:
                    prev = pltpu.roll(t, d, 0)
                    nxt = prev if d == 4 else pltpu.roll(t, 8 - d, 0)
                    new.append(jnp.where(up, jnp.maximum(t, prev), jnp.minimum(t, nxt)))
                v = new
            else:
                d = 1 << (j - 7)
                up = (lane & d) != 0
                other = lane ^ d
                new = []
                for t in v:
                    o = lane_take(t, other)
                    new.append(jnp.where(up, jnp.maximum(t, o), jnp.minimum(t, o)))
                v = new
    return v


def swap_bits(t, sub, lane, p, q):
    sb, lb = (sub >> p) & 1, (lane >> q) & 1
    o = lane_take(t, lane ^ (1 << q))
    o = jnp.where(sb == 1, pltpu.roll(o, 1 << p, 0), pltpu.roll(o, 8 - (1 << p), 0))
    return jnp.where(sb == lb, t, o)


def split(x):
    hi = x.astype(jnp.bfloat16)
    lo = (x - hi.astype(jnp.float32)).astype(jnp.bfloat16)
    return hi, lo


def dot(a, b):
    return lax.dot_general(a, b, (((1,), (0,)), ((), ())), preferred_element_type=jnp.float32)


def prepare_kernel(
    pos_ref, samples_ref, basis_hbm, target_hbm, bits_hbm, keys_ref, ends_ref, own_ref, tab, last,
    basis_ref, target_ref, bits_ref, scratch, sems,
):
    copies = [
        pltpu.make_async_copy(src, dst, sems.at[n])
        for n, (src, dst) in enumerate(
            ((bits_hbm, bits_ref), (target_hbm, target_ref), (basis_hbm, basis_ref))
        )
    ]
    for copy in copies:
        copy.start()

    me, core = pos_ref[0], pos_ref[1]
    sub = lax.broadcasted_iota(jnp.int32, (8, LANES), 0)
    lane = lax.broadcasted_iota(jnp.int32, (8, LANES), 1)
    for c in range(2):
        v = []
        for i in range(16):
            s = samples_ref[i, c]
            s = swap_bits(swap_bits(s, sub, lane, 1, 5), sub, lane, 2, 6)
            p = s & 65535
            place = (((p >> 7) & 1) << 15) | ((p >> 8) << 7) | (p & 127)
            odd = fold((s >> 16) & me)
            r = i * 256 + (sub & 1) * 128 + (sub >> 1) * 32 + (lane & 31)
            v.append((place << 13) | (r << 1) | odd)
        v = bitonic(v, sub, lane)
        for i in range(16):
            scratch[c, pl.ds(i, 8, stride=16), :] = v[i]
        ends_ref[2 * c : 2 * c + 1, :] = scratch[c, 0:1, :] >> 20
        ends_ref[2 * c + 1 : 2 * c + 2, :] = scratch[c, 127:128, :] >> 20
        keys_ref[c * LANES : (c + 1) * LANES, :] = scratch[c].T
    own_ref[...] = scratch[core]

    for copy in copies:
        copy.wait()
    a = lax.broadcasted_iota(jnp.int32, (SIDE, SIDE), 0)
    b = lax.broadcasted_iota(jnp.int32, (SIDE, SIDE), 1)
    walsh = (1 - 2 * fold(a & b)).astype(jnp.float32).astype(jnp.bfloat16)
    flips = [(1 - 2 * bits_ref[pl.ds(bh, SIDE, stride=2), :]).astype(jnp.float32) for bh in range(2)]
    flip = jnp.concatenate(flips, axis=1)
    for k in range(COLS):
        if k < 16:
            base = (k // 8) * 4096 + k % 8
            halves = [basis_ref[pl.ds(base + 8 * bh, SIDE, stride=16), :] for bh in range(2)]
        else:
            halves = [target_ref[pl.ds(bh, SIDE, stride=2), :] for bh in range(2)]
        x = jnp.concatenate(halves, axis=1) * flip
        hi, lo = split(x)
        y = dot(hi, walsh) + dot(lo, walsh)
        hi, lo = split(y)
        z = dot(walsh, hi) + dot(walsh, lo)
        for bh in range(2):
            half = z[:, bh * LANES : (bh + 1) * LANES]
            if k < 16:
                tab[pl.ds(bh * SIDE * 16 + k, SIDE, stride=16), :] = half
            else:
                last[bh * SIDE : (bh + 1) * SIDE, :] = half
    tab[ROWS * 16 :, :] = jnp.zeros(((ROWS_PAD - ROWS) * 16, LANES), jnp.float32)
    last[ROWS:, :] = jnp.zeros((ROWS_PAD - ROWS, LANES), jnp.float32)


VMEM = pl.BlockSpec(memory_space=pltpu.VMEM)
SMEM = pl.BlockSpec(memory_space=pltpu.SMEM)
FAR = pl.BlockSpec(memory_space=pltpu.HBM)
COST = pl.CostEstimate(flops=1_000_000, bytes_accessed=1_000_000, transcendentals=0)


def prepare_call(pos, samples, basis, target, bits):
    return pl.pallas_call(
        prepare_kernel,
        out_shape=(
            jax.ShapeDtypeStruct((256, LANES), jnp.int32),
            jax.ShapeDtypeStruct((4, LANES), jnp.int32),
            jax.ShapeDtypeStruct((LANES, LANES), jnp.int32),
            jax.ShapeDtypeStruct((ROWS_PAD * 16, LANES), jnp.float32),
            jax.ShapeDtypeStruct((ROWS_PAD, LANES), jnp.float32),
        ),
        in_specs=[SMEM, VMEM, FAR, FAR, FAR],
        out_specs=(VMEM,) * 5,
        scratch_shapes=[
            pltpu.VMEM((8192, LANES), jnp.float32),
            pltpu.VMEM((512, LANES), jnp.float32),
            pltpu.VMEM((512, LANES), jnp.int32),
            pltpu.VMEM((2, LANES, LANES), jnp.int32),
            pltpu.SemaphoreType.DMA((3,)),
        ],
        compiler_params=pltpu.CompilerParams(vmem_limit_bytes=24 * 2**20),
        cost_estimate=COST,
        name="sort_and_walsh",
    )(pos, samples, basis, target, bits)


def rank_kernel(own_ref, rank_ref, scratch):
    sub = lax.broadcasted_iota(jnp.int32, (8, LANES), 0)
    lane = lax.broadcasted_iota(jnp.int32, (8, LANES), 1)
    v = []
    for i in range(16):
        key = own_ref[pl.ds(i, 8, stride=16), :]
        slot = (lane & 31) * LANES + sub * 16 + i
        v.append((((key >> 1) & 4095) << 12) | slot)
    v = bitonic(v, sub, lane)
    for i in range(16):
        scratch[pl.ds(i, 8, stride=16), :] = v[i] & 4095
    rank_ref[...] = scratch[...].T


def rank_call(own):
    return pl.pallas_call(
        rank_kernel,
        out_shape=jax.ShapeDtypeStruct((LANES, LANES), jnp.int32),
        in_specs=[VMEM],
        out_specs=VMEM,
        scratch_shapes=[pltpu.VMEM((LANES, LANES), jnp.int32)],
        compiler_params=pltpu.CompilerParams(vmem_limit_bytes=4 * 2**20),
        cost_estimate=COST,
        name="row_rank",
    )(own)


def slots_kernel(scale, off, pos_ref, ends_ref, tab, last, keys_ref, keep, give):
    core = pos_ref[1]
    z = (pos_ref[4] + off) & 3
    sub = lax.broadcasted_iota(jnp.int32, (8, LANES), 0)
    for rel_core, out in enumerate((keep, give)):
        c = core ^ rel_core

        def group(it, _, c=c, out=out):
            lows, tiles, lanes_of, rows_of, subrows, weights = [], [], [], [], [], []
            most, many = jnp.int32(0), jnp.int32(0)
            for q in range(4):
                j = z * 32 + it * 4 + q
                key = jnp.broadcast_to(keys_ref[pl.ds(c * LANES + j, 1), :], (8, LANES))
                low, high = ends_ref[2 * c, j], ends_ref[2 * c + 1, j]
                lows.append(low)
                tiles.append(low >> 3)
                most = jnp.maximum(most, high - low + 1)
                many = jnp.maximum(many, (high >> 3) - (low >> 3) + 1)
                lanes_of.append((key >> 13) & 127)
                rows_of.append((key >> 20) - low)
                subrows.append((key >> 20) - (low >> 3) * 8 - sub)
                weights.append(jnp.where((key & 1) != 0, -scale, scale))

            def add_rows(first, count, eighth, eighths, acc, end=None):
                acc = list(acc)
                for q in range(4):
                    for u in range(count):
                        row = lows[q] + first + u
                        row = row if end is None else jnp.minimum(row, end)
                        hit = rows_of[q] == first + u
                        for t in range(2):
                            tile = tab[pl.ds(pl.multiple_of(row * 16 + 8 * t, 8), 8), :]
                            acc[q * 3 + t] = jnp.where(hit, lane_take(tile, lanes_of[q]), acc[q * 3 + t])
                    for u in range(eighths):
                        row = tiles[q] + eighth + u
                        row = row if end is None else jnp.minimum(row, end // 8)
                        tile = last[pl.ds(pl.multiple_of(row * 8, 8), 8), :]
                        hit = subrows[q] == (eighth + u) * 8
                        acc[q * 3 + 2] = jnp.where(hit, lane_take(tile, lanes_of[q]), acc[q * 3 + 2])
                return tuple(acc)

            acc = add_rows(0, PEEL, 0, EIGHTHS, (jnp.zeros((8, LANES), jnp.float32),) * 12)
            more = (jnp.maximum(most - PEEL, 0) + STEP - 1) // STEP
            more = jnp.maximum(more, many - EIGHTHS)

            def further(n, acc):
                return add_rows(PEEL + n * STEP, STEP, EIGHTHS + n, 1, acc, ROWS - 1)

            acc = lax.fori_loop(0, more, further, acc)
            base = it * (4 * COLS)
            for q in range(4):
                for t in range(2):
                    out[pl.ds(base + q + 32 * t, 8, stride=4), :] = acc[q * 3 + t] * weights[q]
                line = jnp.sum(acc[q * 3 + 2], axis=0, keepdims=True)
                out[pl.ds(base + q + 64, 1), :] = line * weights[q][0:1]
            return 0

        lax.fori_loop(0, 8, group, 0)


def slots_call(scale, off, pos, ends, tab, last, keys):
    part = jax.ShapeDtypeStruct((8 * 4 * COLS, LANES), jnp.float32)
    return pl.pallas_call(
        lambda *refs: slots_kernel(scale, off, *refs),
        out_shape=(part,) * 2,
        in_specs=[SMEM, SMEM, VMEM, VMEM, VMEM],
        out_specs=(VMEM,) * 2,
        compiler_params=pltpu.CompilerParams(vmem_limit_bytes=12 * 2**20),
        cost_estimate=COST,
        name=f"take_slots_{off}",
    )(pos, ends, tab, last, keys)


def order_kernel(rels, pos_ref, rank_ref, *refs):
    parts, outs, table = refs[:4], refs[4:-1], refs[-1]
    y, z = pos_ref[2], pos_ref[4]
    table[...] = (parts[0][...] + parts[1][...]) + (parts[2][...] + parts[3][...])
    rows = 8 * COLS
    at = lax.broadcasted_iota(jnp.int32, (rows, LANES), 0)
    code = (at // (4 * COLS)) * 4 + (at & 3)
    ck = lax.broadcasted_iota(jnp.int32, (24, rows), 0)
    cr = lax.broadcasted_iota(jnp.int32, (24, rows), 1)
    collect = jnp.where((cr % (4 * COLS)) // 4 == ck, 1.0, 0.0).astype(jnp.bfloat16)

    def step(i, _):
        for rel, out in zip(rels, outs):
            line = z * 32 + ((y + rel) & 3) * 8 + i
            slot = jnp.broadcast_to(rank_ref[pl.ds(line, 1), :], (8, LANES))
            index = slot & 127
            pair = slot >> 10
            acc = [jnp.zeros((8, LANES), jnp.float32)] * COLS
            for n in range(4):
                hit = pair == n
                for t in range(COLS):
                    tile = table[n * rows + 8 * t : n * rows + 8 * t + 8, :]
                    acc[t] = jnp.where(hit, lane_take(tile, index), acc[t])
            chosen = jnp.where(code == ((slot >> 7) & 7)[0:1], jnp.concatenate(acc, axis=0), 0.0)
            hi, lo = split(chosen)
            values = dot(collect, hi) + dot(collect, lo)
            for t in range(2):
                out[pl.ds(i + 64 * t, 8, stride=8), :] = values[8 * t : 8 * t + 8]
            out[pl.ds(i + 128, 1), :] = values[16:17]
        return 0

    lax.fori_loop(0, 8, step, 0)


def order_call(rels, pos, rank, parts):
    rows = 8 * COLS
    return pl.pallas_call(
        lambda *refs: order_kernel(rels, *refs),
        out_shape=(jax.ShapeDtypeStruct((rows, LANES), jnp.float32),) * len(rels),
        in_specs=[SMEM] + [VMEM] * 5,
        out_specs=(VMEM,) * len(rels),
        scratch_shapes=[pltpu.VMEM((4 * rows, LANES), jnp.float32)],
        compiler_params=pltpu.CompilerParams(vmem_limit_bytes=8 * 2**20),
        cost_estimate=COST,
        name=f"given_order_{len(rels)}",
    )(pos, rank, *parts)


def finish_kernel(factor, pos_ref, owners_ref, p0, p1, p2, p3, sketch, gram, table):
    core, y, x, z = pos_ref[1], pos_ref[2], pos_ref[3], pos_ref[4]
    table[0 : 8 * COLS, :] = (p0[...] + p1[...]) + (p2[...] + p3[...])
    table[8 * COLS :, :] = jnp.zeros((24 * 8 - 8 * COLS, LANES), jnp.float32)
    for h in range(2):
        sketch[:, h * LANES : (h + 1) * LANES] = table[pl.ds(2 * x + h, 24, stride=8), :][:COLS]
    pieces, lefts = [], []
    for tx in range(4):
        for h in range(2):
            v = table[pl.ds(2 * tx + h, 24, stride=8), :]
            owner = owners_ref[y * 4 + tx, core, pl.ds(2 * z + h, 1), :]
            lefts.append(jnp.concatenate([jnp.where(owner == g, v[:16], 0.0) for g in range(GROUPS)], axis=0))
            pieces.append(v)
    value = jnp.concatenate(pieces, axis=1)
    left = jnp.concatenate(lefts, axis=1)
    total = lax.dot_general(
        value, left, (((1,), (1,)), ((), ())),
        precision=lax.Precision.HIGHEST, preferred_element_type=jnp.float32,
    )
    total = factor * total
    for to in range(4):
        own = [total[8 * n : 8 * n + 8, 32 * to : 32 * to + 32] for n in range(3)]
        message = jnp.concatenate(own + [jnp.zeros((8, 32), jnp.float32)], axis=1)
        for row in range(4):
            gram[row * 4 + to] = message


def finish_call(factor, pos, owners, parts):
    return pl.pallas_call(
        lambda *refs: finish_kernel(factor, *refs),
        out_shape=(
            jax.ShapeDtypeStruct((COLS, SIDE), jnp.float32),
            jax.ShapeDtypeStruct((16, 8, LANES), jnp.float32),
        ),
        in_specs=[SMEM] + [VMEM] * 5,
        out_specs=(VMEM,) * 2,
        scratch_shapes=[pltpu.VMEM((24 * 8, LANES), jnp.float32)],
        compiler_params=pltpu.CompilerParams(vmem_limit_bytes=8 * 2**20),
        name="rows_and_gram",
    )(pos, owners, *parts)


def gram_kernel(a, b, out):
    total = a[...] + b[...]
    total = jnp.concatenate([total[:, 32 * n : 32 * n + 32] for n in range(3)], axis=0).T
    for g in range(2):
        out[g] = total[16 * g : 16 * g + 16, :COLS]


def gram_call(a, b):
    return pl.pallas_call(
        gram_kernel,
        out_shape=jax.ShapeDtypeStruct((2, 16, COLS), jnp.float32),
        in_specs=[VMEM] * 2,
        out_specs=VMEM,
        compiler_params=pltpu.CompilerParams(vmem_limit_bytes=4 * 2**20),
        name="own_gram",
    )(a, b)


def send(v, axis, off):
    return lax.ppermute(v, AXES, shift(axis, off))


def planes():
    return [[number(y, x, c, z) for y in range(4) for z in range(4)] for x in range(4) for c in range(2)]


def shards(basis, target, sign_bits, samples, owners):
    rows = basis.shape[1]
    total_samples = samples.shape[0]
    scale = 1.0 / math.sqrt(rows * 128)
    wide = lax.axis_index("wide")
    z = lax.axis_index("quad")
    core, x, y = wide & 1, (wide >> 1) & 3, wide >> 3
    pos = jnp.stack([wide * 4 + z, core, y, x, z, z, z, z]).astype(jnp.int32)

    tiles = basis.reshape(2, 8, 512, LANES).transpose(0, 2, 1, 3).reshape(8192, LANES)
    far = [tiles, target.reshape(512, LANES), sign_bits.reshape(512, LANES)]
    far = [pltpu.with_memory_space_constraint(v, pltpu.HBM) for v in far]
    keys, ends, own, tab, last = prepare_call(pos, samples.reshape(16, 2, 8, LANES), *far)
    parts, held = [], []
    for n, off in enumerate((2, 1, 3, 0)):
        if n >= 2:
            keys, held[n - 2] = lax.optimization_barrier((keys, held[n - 2]))
        keep, give = slots_call(scale, off, pos, ends, tab, last, keys)
        held.append(keep + send(give, "c", 1))
        if n >= 2:
            parts.append(send(held[n - 2], "z", (2, 1)[n - 2]))
    own, keep = lax.optimization_barrier((own, keep))
    rank = rank_call(own)
    parts += [send(held[2], "z", 3), held[3]]
    lines = order_call((2, 1, 3), pos, rank, parts)
    line = order_call((0,), pos, rank, parts)[0]
    line = (line + send(lines[0], "y", 2)) + (send(lines[1], "y", 1) + send(lines[2], "y", 3))
    around = [line] + [send(line, "x", off) for off in (2, 1, 3)]
    sketch, gram = finish_call(GROUPS / total_samples, pos, owners.reshape(16, 2, 8, LANES), around)
    gram = lax.all_to_all(gram, AXES, 0, 0, tiled=True, axis_index_groups=planes())
    gram = jnp.sum(gram, axis=0)
    return sketch.T, gram_call(gram, send(gram, "c", 1))


def solution(mesh):
    placed = (P(None, AXES), P(AXES), P(AXES), P(), P())
    return jax.shard_map(
        shards,
        mesh=mesh,
        in_specs=placed,
        out_specs=(P(AXES, None), P("quad", None, None)),
        check_vma=False,
    )
```

```python
import math

import jax
import jax.numpy as jnp
from jax import lax
from jax.experimental import pallas as pl
from jax.experimental.pallas import tpu as pltpu
from jax.sharding import PartitionSpec as P

GROUPS = 8
AXES = ("wide", "quad")
LANES = 128
COLS = 17
SIDE = 256
PEEL = 20
STEP = 4
EIGHTHS = 4
ROWS = 512
ROWS_PAD = 536


def number(y, x, c, z):
    return ((y * 4 + x) * 2 + c) * 4 + z


def shift(axis, off):
    pairs = []
    for y in range(4):
        for x in range(4):
            for c in range(2):
                for z in range(4):
                    at = {"y": y, "x": x, "c": c, "z": z}
                    size = 2 if axis == "c" else 4
                    to = dict(at)
                    to[axis] = (at[axis] + off) % size
                    pairs.append((number(**at), number(**to)))
    return pairs


def fold(v):
    v = v ^ (v >> 8)
    v = v ^ (v >> 4)
    v = v ^ (v >> 2)
    v = v ^ (v >> 1)
    return v & 1


def lane_take(tile, index):
    return jnp.take_along_axis(tile, index, axis=1)


def bitonic_steps(v, sub, lane):
    for k in range(1, 13):
        for b in (k - 1, k):
            if b == 0 or b == 12:
                continue
            if b < 4:
                v[:] = [~t if (i >> b) & 1 else t for i, t in enumerate(v)]
            else:
                bit = (sub >> (b - 4)) if b < 7 else (lane >> (b - 7))
                m = -(bit & 1)
                v[:] = [t ^ m for t in v]
        for j in range(k - 1, -1, -1):
            if j < 4:
                new = list(v)
                for i in range(16):
                    if not (i >> j) & 1:
                        a, b = v[i], v[i | (1 << j)]
                        new[i] = jnp.minimum(a, b)
                        new[i | (1 << j)] = jnp.maximum(a, b)
                v[:] = new
            elif j < 7:
                d = 1 << (j - 4)
                up = (sub & d) != 0
                new = []
                for t in v:
                    prev = pltpu.roll(t, d, 0)
                    nxt = prev if d == 4 else pltpu.roll(t, 8 - d, 0)
                    new.append(jnp.where(up, jnp.maximum(t, prev), jnp.minimum(t, nxt)))
                v[:] = new
            else:
                d = 1 << (j - 7)
                up = (lane & d) != 0
                other = lane ^ d
                new = []
                for t in v:
                    o = lane_take(t, other)
                    new.append(jnp.where(up, jnp.maximum(t, o), jnp.minimum(t, o)))
                v[:] = new
            yield


def bitonic(v, sub, lane):
    for _ in bitonic_steps(v, sub, lane):
        pass
    return v


def swap_bits(t, sub, lane, p, q):
    sb, lb = (sub >> p) & 1, (lane >> q) & 1
    o = lane_take(t, lane ^ (1 << q))
    o = jnp.where(sb == 1, pltpu.roll(o, 1 << p, 0), pltpu.roll(o, 8 - (1 << p), 0))
    return jnp.where(sb == lb, t, o)


def split(x):
    hi = x.astype(jnp.bfloat16)
    lo = (x - hi.astype(jnp.float32)).astype(jnp.bfloat16)
    return hi, lo


def dot(a, b):
    return lax.dot_general(a, b, (((1,), (0,)), ((), ())), preferred_element_type=jnp.float32)


def prepare_kernel(
    pos_ref, samples_ref, basis_hbm, target_hbm, bits_hbm, keys_ref, ends_ref, own_ref, tab, last,
    basis_ref, target_ref, bits_ref, scratch, walsh_ref, flip_ref, sems,
):
    copies = [
        pltpu.make_async_copy(src, dst, sems.at[n])
        for n, (src, dst) in enumerate(
            ((bits_hbm, bits_ref), (target_hbm, target_ref), (basis_hbm, basis_ref))
        )
    ]
    for copy in copies:
        copy.start()

    me, core = pos_ref[0], pos_ref[1]
    sub = lax.broadcasted_iota(jnp.int32, (8, LANES), 0)
    lane = lax.broadcasted_iota(jnp.int32, (8, LANES), 1)
    def load(c):
        v = []
        for i in range(16):
            s = samples_ref[i, c]
            s = swap_bits(swap_bits(s, sub, lane, 1, 5), sub, lane, 2, 6)
            p = s & 65535
            place = (((p >> 7) & 1) << 15) | ((p >> 8) << 7) | (p & 127)
            odd = fold((s >> 16) & me)
            r = i * 256 + (sub & 1) * 128 + (sub >> 1) * 32 + (lane & 31)
            v.append((place << 13) | (r << 1) | odd)
        return v

    def store(c, v):
        for i in range(16):
            scratch[c, pl.ds(i, 8, stride=16), :] = v[i]
        ends_ref[2 * c : 2 * c + 1, :] = scratch[c, 0:1, :] >> 20
        ends_ref[2 * c + 1 : 2 * c + 2, :] = scratch[c, 127:128, :] >> 20
        keys_ref[c * LANES : (c + 1) * LANES, :] = scratch[c].T

    def flips_of(bh):
        return (1 - 2 * bits_ref[pl.ds(bh, SIDE, stride=2), :]).astype(jnp.float32)

    def mix(k):
        if k < 16:
            base = (k // 8) * 4096 + k % 8
            halves = [basis_ref[pl.ds(base + 8 * bh, SIDE, stride=16), :] for bh in range(2)]
        else:
            halves = [target_ref[pl.ds(bh, SIDE, stride=2), :] for bh in range(2)]
        x = jnp.concatenate(halves, axis=1) * flip_ref[...]
        hi, lo = split(x)
        walsh = walsh_ref[...]
        y = dot(hi, walsh) + dot(lo, walsh)
        hi, lo = split(y)
        z = dot(walsh, hi) + dot(walsh, lo)
        for bh in range(2):
            half = z[:, bh * LANES : (bh + 1) * LANES]
            if k < 16:
                tab[pl.ds(bh * SIDE * 16 + k, SIDE, stride=16), :] = half
            else:
                last[bh * SIDE : (bh + 1) * SIDE, :] = half

    a = lax.broadcasted_iota(jnp.int32, (SIDE, SIDE), 0)
    b = lax.broadcasted_iota(jnp.int32, (SIDE, SIDE), 1)
    walsh_ref[...] = (1 - 2 * fold(a & b)).astype(jnp.float32).astype(jnp.bfloat16)
    store(0, bitonic(load(0), sub, lane))
    for copy in copies:
        copy.wait()
    flip_ref[...] = jnp.concatenate([flips_of(0), flips_of(1)], axis=1)
    v = load(1)
    todo = list(range(COLS))
    for n, _ in enumerate(bitonic_steps(v, sub, lane)):
        if n % 5 == 0 and todo:
            mix(todo.pop(0))
    while todo:
        mix(todo.pop(0))
    store(1, v)
    own_ref[...] = scratch[core]
    tab[ROWS * 16 :, :] = jnp.zeros(((ROWS_PAD - ROWS) * 16, LANES), jnp.float32)
    last[ROWS:, :] = jnp.zeros((ROWS_PAD - ROWS, LANES), jnp.float32)


VMEM = pl.BlockSpec(memory_space=pltpu.VMEM)
SMEM = pl.BlockSpec(memory_space=pltpu.SMEM)
FAR = pl.BlockSpec(memory_space=pltpu.HBM)
COST = pl.CostEstimate(flops=1_000_000, bytes_accessed=1_000_000, transcendentals=0)


def prepare_call(pos, samples, basis, target, bits):
    return pl.pallas_call(
        prepare_kernel,
        out_shape=(
            jax.ShapeDtypeStruct((256, LANES), jnp.int32),
            jax.ShapeDtypeStruct((4, LANES), jnp.int32),
            jax.ShapeDtypeStruct((LANES, LANES), jnp.int32),
            jax.ShapeDtypeStruct((ROWS_PAD * 16, LANES), jnp.float32),
            jax.ShapeDtypeStruct((ROWS_PAD, LANES), jnp.float32),
        ),
        in_specs=[SMEM, VMEM, FAR, FAR, FAR],
        out_specs=(VMEM,) * 5,
        scratch_shapes=[
            pltpu.VMEM((8192, LANES), jnp.float32),
            pltpu.VMEM((512, LANES), jnp.float32),
            pltpu.VMEM((512, LANES), jnp.int32),
            pltpu.VMEM((2, LANES, LANES), jnp.int32),
            pltpu.VMEM((SIDE, SIDE), jnp.bfloat16),
            pltpu.VMEM((SIDE, SIDE), jnp.float32),
            pltpu.SemaphoreType.DMA((3,)),
        ],
        compiler_params=pltpu.CompilerParams(vmem_limit_bytes=24 * 2**20),
        cost_estimate=COST,
        name="sort_and_walsh",
    )(pos, samples, basis, target, bits)


def rank_kernel(own_ref, rank_ref, scratch):
    sub = lax.broadcasted_iota(jnp.int32, (8, LANES), 0)
    lane = lax.broadcasted_iota(jnp.int32, (8, LANES), 1)
    v = []
    for i in range(16):
        key = own_ref[pl.ds(i, 8, stride=16), :]
        slot = (lane & 31) * LANES + sub * 16 + i
        v.append((((key >> 1) & 4095) << 12) | slot)
    v = bitonic(v, sub, lane)
    for i in range(16):
        scratch[pl.ds(i, 8, stride=16), :] = v[i] & 4095
    rank_ref[...] = scratch[...].T


def rank_call(own):
    return pl.pallas_call(
        rank_kernel,
        out_shape=jax.ShapeDtypeStruct((LANES, LANES), jnp.int32),
        in_specs=[VMEM],
        out_specs=VMEM,
        scratch_shapes=[pltpu.VMEM((LANES, LANES), jnp.int32)],
        compiler_params=pltpu.CompilerParams(vmem_limit_bytes=4 * 2**20),
        cost_estimate=COST,
        name="row_rank",
    )(own)


def slots_kernel(scale, off, cores, pos_ref, ends_ref, tab, last, keys_ref, *outs):
    core = pos_ref[1]
    z = (pos_ref[4] + off) & 3
    sub = lax.broadcasted_iota(jnp.int32, (8, LANES), 0)
    for rel_core, out in zip(cores, outs):
        c = core ^ rel_core

        def group(it, _, c=c, out=out):
            lows, tiles, lanes_of, rows_of, subrows, weights = [], [], [], [], [], []
            most, many = jnp.int32(0), jnp.int32(0)
            for q in range(4):
                j = z * 32 + it * 4 + q
                key = jnp.broadcast_to(keys_ref[pl.ds(c * LANES + j, 1), :], (8, LANES))
                low, high = ends_ref[2 * c, j], ends_ref[2 * c + 1, j]
                lows.append(low)
                tiles.append(low >> 3)
                most = jnp.maximum(most, high - low + 1)
                many = jnp.maximum(many, (high >> 3) - (low >> 3) + 1)
                lanes_of.append((key >> 13) & 127)
                rows_of.append((key >> 20) - low)
                subrows.append((key >> 20) - (low >> 3) * 8 - sub)
                weights.append(jnp.where((key & 1) != 0, -scale, scale))

            def add_rows(first, count, eighth, eighths, acc, end=None):
                acc = list(acc)
                for q in range(4):
                    for u in range(count):
                        row = lows[q] + first + u
                        row = row if end is None else jnp.minimum(row, end)
                        hit = rows_of[q] == first + u
                        for t in range(2):
                            tile = tab[pl.ds(pl.multiple_of(row * 16 + 8 * t, 8), 8), :]
                            acc[q * 3 + t] = jnp.where(hit, lane_take(tile, lanes_of[q]), acc[q * 3 + t])
                    for u in range(eighths):
                        row = tiles[q] + eighth + u
                        row = row if end is None else jnp.minimum(row, end // 8)
                        tile = last[pl.ds(pl.multiple_of(row * 8, 8), 8), :]
                        hit = subrows[q] == (eighth + u) * 8
                        acc[q * 3 + 2] = jnp.where(hit, lane_take(tile, lanes_of[q]), acc[q * 3 + 2])
                return tuple(acc)

            acc = add_rows(0, PEEL, 0, EIGHTHS, (jnp.zeros((8, LANES), jnp.float32),) * 12)
            more = (jnp.maximum(most - PEEL, 0) + STEP - 1) // STEP
            more = jnp.maximum(more, many - EIGHTHS)

            def further(n, acc):
                return add_rows(PEEL + n * STEP, STEP, EIGHTHS + n, 1, acc, ROWS - 1)

            acc = lax.fori_loop(0, more, further, acc)
            base = it * (4 * COLS)
            for q in range(4):
                for t in range(2):
                    out[pl.ds(base + q + 32 * t, 8, stride=4), :] = acc[q * 3 + t] * weights[q]
                line = jnp.sum(acc[q * 3 + 2], axis=0, keepdims=True)
                out[pl.ds(base + q + 64, 1), :] = line * weights[q][0:1]
            return 0

        lax.fori_loop(0, 8, group, 0)


def slots_call(scale, off, cores, pos, ends, tab, last, keys):
    part = jax.ShapeDtypeStruct((8 * 4 * COLS, LANES), jnp.float32)
    return pl.pallas_call(
        lambda *refs: slots_kernel(scale, off, cores, *refs),
        out_shape=(part,) * len(cores),
        in_specs=[SMEM, SMEM, VMEM, VMEM, VMEM],
        out_specs=(VMEM,) * len(cores),
        compiler_params=pltpu.CompilerParams(vmem_limit_bytes=12 * 2**20),
        cost_estimate=COST,
        name=f"take_slots_{off}" + "".join(map(str, cores)),
    )(pos, ends, tab, last, keys)


def order_lines(rel, pos_ref, rank_ref, table, out, boxes):
    y, z = pos_ref[2], pos_ref[4]
    rows = 8 * COLS
    at = lax.broadcasted_iota(jnp.int32, (rows, LANES), 0)
    code = jnp.where(at >= rows // 2, 4, 0) + (at & 3)
    for i in range(8):
        line = z * 32 + ((y + rel) & 3) * 8 + i
        slot = jnp.broadcast_to(rank_ref[pl.ds(line, 1), :], (8, LANES))
        index = slot & 127
        pair = slot >> 10
        acc = [jnp.zeros((8, LANES), jnp.float32)] * COLS
        for n in range(4):
            hit = pair == n
            for t in range(COLS):
                tile = table[n * rows + 8 * t : n * rows + 8 * t + 8, :]
                acc[t] = jnp.where(hit, lane_take(tile, index), acc[t])
        boxes[i] = jnp.where(code == ((slot >> 7) & 7)[0:1], jnp.concatenate(acc, axis=0), 0.0)
        starts = [half * (rows // 2) + q for half in range(2) for q in range(4)]
        values = sum(boxes[i, pl.ds(first, 16, stride=4), :] for first in starts)
        for t in range(2):
            out[pl.ds(i + 64 * t, 8, stride=8), :] = values[8 * t : 8 * t + 8]
        out[128 + i : 129 + i, :] = sum(boxes[i, first + 64 : first + 65, :] for first in starts)


def order_first_kernel(rels, pos_ref, rank_ref, p0, p1, p2, p3, table, *refs):
    table[...] = (p0[...] + p1[...]) + (p2[...] + p3[...])
    for rel, out in zip(rels, refs):
        order_lines(rel, pos_ref, rank_ref, table, out, refs[-1])


def order_call(rel, pos, rank, *given):
    rows = 8 * COLS
    out = jax.ShapeDtypeStruct((rows, LANES), jnp.float32)
    table = jax.ShapeDtypeStruct((4 * rows, LANES), jnp.float32)
    first = len(given) > 1
    kernel = order_first_kernel if first else order_lines
    return pl.pallas_call(
        lambda *refs: kernel(rel, *refs),
        out_shape=(table,) + (out,) * len(rel) if first else out,
        in_specs=[SMEM] + [VMEM] * (1 + len(given)),
        out_specs=(VMEM,) * (1 + len(rel)) if first else VMEM,
        scratch_shapes=[pltpu.VMEM((8, rows, LANES), jnp.float32)],
        compiler_params=pltpu.CompilerParams(vmem_limit_bytes=8 * 2**20),
        cost_estimate=COST,
        name="given_order_far" if first else "given_order_own",
    )(pos, rank, *given)


def finish_kernel(factor, pos_ref, owners_ref, p0, p1, p2, p3, sketch, gram, table):
    core, y, x, z = pos_ref[1], pos_ref[2], pos_ref[3], pos_ref[4]
    table[0 : 8 * COLS, :] = (p0[...] + p1[...]) + (p2[...] + p3[...])
    table[8 * COLS :, :] = jnp.zeros((24 * 8 - 8 * COLS, LANES), jnp.float32)
    for h in range(2):
        sketch[:, h * LANES : (h + 1) * LANES] = table[pl.ds(2 * x + h, 24, stride=8), :][:COLS]
    pieces, lefts = [], []
    for tx in range(4):
        for h in range(2):
            v = table[pl.ds(2 * tx + h, 24, stride=8), :]
            owner = owners_ref[y * 4 + tx, core, pl.ds(2 * z + h, 1), :]
            lefts.append(jnp.concatenate([jnp.where(owner == g, v[:16], 0.0) for g in range(GROUPS)], axis=0))
            pieces.append(v)
    value = jnp.concatenate(pieces, axis=1)
    left = jnp.concatenate(lefts, axis=1)
    total = lax.dot_general(
        value, left, (((1,), (1,)), ((), ())),
        precision=lax.Precision.HIGHEST, preferred_element_type=jnp.float32,
    )
    total = factor * total
    for to in range(4):
        own = [total[8 * n : 8 * n + 8, 32 * to : 32 * to + 32] for n in range(3)]
        message = jnp.concatenate(own + [jnp.zeros((8, 32), jnp.float32)], axis=1)
        for row in range(4):
            gram[row * 4 + to] = message


def finish_call(factor, pos, owners, parts):
    return pl.pallas_call(
        lambda *refs: finish_kernel(factor, *refs),
        out_shape=(
            jax.ShapeDtypeStruct((COLS, SIDE), jnp.float32),
            jax.ShapeDtypeStruct((16, 8, LANES), jnp.float32),
        ),
        in_specs=[SMEM] + [VMEM] * 5,
        out_specs=(VMEM,) * 2,
        scratch_shapes=[pltpu.VMEM((24 * 8, LANES), jnp.float32)],
        compiler_params=pltpu.CompilerParams(vmem_limit_bytes=8 * 2**20),
        name="rows_and_gram",
    )(pos, owners, *parts)


def gram_kernel(a, b, out):
    total = a[...] + b[...]
    total = jnp.concatenate([total[:, 32 * n : 32 * n + 32] for n in range(3)], axis=0).T
    for g in range(2):
        out[g] = total[16 * g : 16 * g + 16, :COLS]


def gram_call(a, b):
    return pl.pallas_call(
        gram_kernel,
        out_shape=jax.ShapeDtypeStruct((2, 16, COLS), jnp.float32),
        in_specs=[VMEM] * 2,
        out_specs=VMEM,
        compiler_params=pltpu.CompilerParams(vmem_limit_bytes=4 * 2**20),
        name="own_gram",
    )(a, b)


def send(v, axis, off):
    return lax.ppermute(v, AXES, shift(axis, off))


def planes():
    return [[number(y, x, c, z) for y in range(4) for z in range(4)] for x in range(4) for c in range(2)]


def shards(basis, target, sign_bits, samples, owners):
    rows = basis.shape[1]
    total_samples = samples.shape[0]
    scale = 1.0 / math.sqrt(rows * 128)
    wide = lax.axis_index("wide")
    z = lax.axis_index("quad")
    core, x, y = wide & 1, (wide >> 1) & 3, wide >> 3
    pos = jnp.stack([wide * 4 + z, core, y, x, z, z, z, z]).astype(jnp.int32)

    tiles = basis.reshape(2, 8, 512, LANES).transpose(0, 2, 1, 3).reshape(8192, LANES)
    far = [tiles, target.reshape(512, LANES), sign_bits.reshape(512, LANES)]
    far = [pltpu.with_memory_space_constraint(v, pltpu.HBM) for v in far]
    keys, ends, own, tab, last = prepare_call(pos, samples.reshape(16, 2, 8, LANES), *far)
    def after(v, *others):
        return lax.optimization_barrier((v,) + others)[0]

    def take(off, *cores):
        return slots_call(scale, off, cores, pos, ends, tab, last, keys)

    keep2, give2 = take(2, 0, 1)
    got2 = send(give2, "c", 1)
    give1, = take(1, 1)
    got1 = send(give1, "c", 1)
    both2 = keep2 + got2
    keys = after(keys, give1, both2)
    keep1, = take(1, 0)
    both1 = keep1 + got1
    keys = after(keys, both1)
    give3, = take(3, 1)
    got3 = send(give3, "c", 1)
    part2 = send(both2, "z", 2)
    keys = after(keys, give3, part2)
    keep3, = take(3, 0)
    both3 = keep3 + got3
    part1 = send(both1, "z", 1)
    part3 = send(both3, "z", 3)
    keys = after(keys, both3)
    keep, give = take(0, 0, 1)
    rank = rank_call(after(own, keep, part1, part3))
    parts = [part2, part1, part3, keep + send(give, "c", 1)]
    rels = (2, 1, 3)
    table, *lines = order_call(rels, pos, rank, *parts)
    got = [send(line, "y", rel) for line, rel in zip(lines, rels)]
    line = (order_call(0, pos, rank, table) + got[0]) + (got[1] + got[2])
    around = [line] + [send(line, "x", off) for off in (2, 1, 3)]
    sketch, gram = finish_call(GROUPS / total_samples, pos, owners.reshape(16, 2, 8, LANES), around)
    gram = lax.all_to_all(gram, AXES, 0, 0, tiled=True, axis_index_groups=planes())
    gram = jnp.sum(gram, axis=0)
    return sketch.T, gram_call(gram, send(gram, "c", 1))


def solution(mesh):
    placed = (P(None, AXES), P(AXES), P(AXES), P(), P())
    return jax.shard_map(
        shards,
        mesh=mesh,
        in_specs=placed,
        out_specs=(P(AXES, None), P("quad", None, None)),
        check_vma=False,
    )
```

```python
import math

import jax
import jax.numpy as jnp
from jax import lax
from jax.experimental import pallas as pl
from jax.experimental.pallas import tpu as pltpu
from jax.sharding import PartitionSpec as P

GROUPS = 8
AXES = ("wide", "quad")
LANES = 128
COLS = 17
SIDE = 256
PEEL = 20
STEP = 4
EIGHTHS = 4
ROWS = 512
ROWS_PAD = 536


def number(y, x, c, z):
    return ((y * 4 + x) * 2 + c) * 4 + z


def shift(axis, off):
    pairs = []
    for y in range(4):
        for x in range(4):
            for c in range(2):
                for z in range(4):
                    at = {"y": y, "x": x, "c": c, "z": z}
                    size = 2 if axis == "c" else 4
                    to = dict(at)
                    to[axis] = (at[axis] + off) % size
                    pairs.append((number(**at), number(**to)))
    return pairs


def fold(v):
    v = v ^ (v >> 8)
    v = v ^ (v >> 4)
    v = v ^ (v >> 2)
    v = v ^ (v >> 1)
    return v & 1


def lane_take(tile, index):
    return jnp.take_along_axis(tile, index, axis=1)


def bitonic_steps(v, sub, lane):
    for k in range(1, 13):
        for b in (k - 1, k):
            if b == 0 or b == 12:
                continue
            if b < 4:
                v[:] = [~t if (i >> b) & 1 else t for i, t in enumerate(v)]
            else:
                bit = (sub >> (b - 4)) if b < 7 else (lane >> (b - 7))
                m = -(bit & 1)
                v[:] = [t ^ m for t in v]
        for j in range(k - 1, -1, -1):
            if j < 4:
                new = list(v)
                for i in range(16):
                    if not (i >> j) & 1:
                        a, b = v[i], v[i | (1 << j)]
                        new[i] = jnp.minimum(a, b)
                        new[i | (1 << j)] = jnp.maximum(a, b)
                v[:] = new
            elif j < 7:
                d = 1 << (j - 4)
                up = (sub & d) != 0
                new = []
                for t in v:
                    prev = pltpu.roll(t, d, 0)
                    nxt = prev if d == 4 else pltpu.roll(t, 8 - d, 0)
                    new.append(jnp.where(up, jnp.maximum(t, prev), jnp.minimum(t, nxt)))
                v[:] = new
            else:
                d = 1 << (j - 7)
                up = (lane & d) != 0
                other = lane ^ d
                new = []
                for t in v:
                    o = lane_take(t, other)
                    new.append(jnp.where(up, jnp.maximum(t, o), jnp.minimum(t, o)))
                v[:] = new
            yield


def bitonic(v, sub, lane):
    for _ in bitonic_steps(v, sub, lane):
        pass
    return v


def swap_bits(t, sub, lane, p, q):
    sb, lb = (sub >> p) & 1, (lane >> q) & 1
    o = lane_take(t, lane ^ (1 << q))
    o = jnp.where(sb == 1, pltpu.roll(o, 1 << p, 0), pltpu.roll(o, 8 - (1 << p), 0))
    return jnp.where(sb == lb, t, o)


def split(x):
    hi = x.astype(jnp.bfloat16)
    lo = (x - hi.astype(jnp.float32)).astype(jnp.bfloat16)
    return hi, lo


def dot(a, b):
    return lax.dot_general(a, b, (((1,), (0,)), ((), ())), preferred_element_type=jnp.float32)


def prepare_kernel(
    pos_ref, samples_hbm, basis_hbm, target_hbm, bits_hbm, keys_ref, ends_ref, rank_ref, tab, last,
    samples_ref, basis_ref, target_ref, bits_ref, scratch, walsh_ref, flip_ref, sems,
):
    copies = [
        pltpu.make_async_copy(src, dst, sems.at[n])
        for n, (src, dst) in enumerate(
            ((samples_hbm, samples_ref), (bits_hbm, bits_ref), (target_hbm, target_ref), (basis_hbm, basis_ref))
        )
    ]
    for copy in copies:
        copy.start()

    me, core = pos_ref[0], pos_ref[1]
    sub = lax.broadcasted_iota(jnp.int32, (8, LANES), 0)
    lane = lax.broadcasted_iota(jnp.int32, (8, LANES), 1)
    def load(c):
        v = []
        for i in range(16):
            s = samples_ref[i, c]
            s = swap_bits(swap_bits(s, sub, lane, 1, 5), sub, lane, 2, 6)
            p = s & 65535
            place = (((p >> 7) & 1) << 15) | ((p >> 8) << 7) | (p & 127)
            odd = fold((s >> 16) & me)
            r = i * 256 + (sub & 1) * 128 + (sub >> 1) * 32 + (lane & 31)
            v.append((place << 13) | (r << 1) | odd)
        return v

    def store(c, v):
        for i in range(16):
            scratch[c, pl.ds(i, 8, stride=16), :] = v[i]
        ends_ref[2 * c : 2 * c + 1, :] = scratch[c, 0:1, :] >> 20
        ends_ref[2 * c + 1 : 2 * c + 2, :] = scratch[c, 127:128, :] >> 20
        keys_ref[c * LANES : (c + 1) * LANES, :] = scratch[c].T

    def flips_of(bh):
        return (1 - 2 * bits_ref[pl.ds(bh, SIDE, stride=2), :]).astype(jnp.float32)

    def mix(k):
        if k < 16:
            base = (k // 8) * 4096 + k % 8
            halves = [basis_ref[pl.ds(base + 8 * bh, SIDE, stride=16), :] for bh in range(2)]
        else:
            halves = [target_ref[pl.ds(bh, SIDE, stride=2), :] for bh in range(2)]
        x = jnp.concatenate(halves, axis=1) * flip_ref[...]
        hi, lo = split(x)
        walsh = walsh_ref[...]
        y = dot(hi, walsh) + dot(lo, walsh)
        hi, lo = split(y)
        z = dot(walsh, hi) + dot(walsh, lo)
        for bh in range(2):
            half = z[:, bh * LANES : (bh + 1) * LANES]
            if k < 16:
                tab[pl.ds(bh * SIDE * 16 + k, SIDE, stride=16), :] = half
            else:
                last[bh * SIDE : (bh + 1) * SIDE, :] = half

    a = lax.broadcasted_iota(jnp.int32, (SIDE, SIDE), 0)
    b = lax.broadcasted_iota(jnp.int32, (SIDE, SIDE), 1)
    walsh_ref[...] = (1 - 2 * fold(a & b)).astype(jnp.float32).astype(jnp.bfloat16)
    copies[0].wait()
    store(0, bitonic(load(0), sub, lane))
    for copy in copies[1:]:
        copy.wait()
    flip_ref[...] = jnp.concatenate([flips_of(0), flips_of(1)], axis=1)
    v = load(1)
    todo = list(range(COLS))
    for n, _ in enumerate(bitonic_steps(v, sub, lane)):
        if n % 9 == 0:
            mix(todo.pop(0))
    store(1, v)
    v = []
    for i in range(16):
        key = scratch[core, pl.ds(i, 8, stride=16), :]
        slot = (lane & 31) * LANES + sub * 16 + i
        v.append((((key >> 1) & 4095) << 12) | slot)
    for n, _ in enumerate(bitonic_steps(v, sub, lane)):
        if n % 9 == 0 and todo:
            mix(todo.pop(0))
    for i in range(16):
        scratch[2, pl.ds(i, 8, stride=16), :] = v[i] & 4095
    rank_ref[...] = scratch[2].T
    tab[ROWS * 16 :, :] = jnp.zeros(((ROWS_PAD - ROWS) * 16, LANES), jnp.float32)
    last[ROWS:, :] = jnp.zeros((ROWS_PAD - ROWS, LANES), jnp.float32)


VMEM = pl.BlockSpec(memory_space=pltpu.VMEM)
SMEM = pl.BlockSpec(memory_space=pltpu.SMEM)
FAR = pl.BlockSpec(memory_space=pltpu.HBM)
COST = pl.CostEstimate(flops=1_000_000, bytes_accessed=1_000_000, transcendentals=0)


def prepare_call(pos, samples, basis, target, bits):
    return pl.pallas_call(
        prepare_kernel,
        out_shape=(
            jax.ShapeDtypeStruct((256, LANES), jnp.int32),
            jax.ShapeDtypeStruct((4, LANES), jnp.int32),
            jax.ShapeDtypeStruct((LANES, LANES), jnp.int32),
            jax.ShapeDtypeStruct((ROWS_PAD * 16, LANES), jnp.float32),
            jax.ShapeDtypeStruct((ROWS_PAD, LANES), jnp.float32),
        ),
        in_specs=[SMEM, FAR, FAR, FAR, FAR],
        out_specs=(VMEM,) * 5,
        scratch_shapes=[
            pltpu.VMEM((16, 2, 8, LANES), jnp.int32),
            pltpu.VMEM((8192, LANES), jnp.float32),
            pltpu.VMEM((512, LANES), jnp.float32),
            pltpu.VMEM((512, LANES), jnp.int32),
            pltpu.VMEM((3, LANES, LANES), jnp.int32),
            pltpu.VMEM((SIDE, SIDE), jnp.bfloat16),
            pltpu.VMEM((SIDE, SIDE), jnp.float32),
            pltpu.SemaphoreType.DMA((4,)),
        ],
        compiler_params=pltpu.CompilerParams(vmem_limit_bytes=24 * 2**20),
        cost_estimate=COST,
        name="sort_and_walsh",
    )(pos, samples, basis, target, bits)


def slots_kernel(scale, off, cores, pos_ref, ends_ref, tab, last, keys_ref, *outs):
    core = pos_ref[1]
    z = (pos_ref[4] + off) & 3
    sub = lax.broadcasted_iota(jnp.int32, (8, LANES), 0)
    for rel_core, out in zip(cores, outs):
        c = core ^ rel_core

        def group(it, _, c=c, out=out):
            lows, tiles, lanes_of, rows_of, subrows, weights = [], [], [], [], [], []
            most, many = jnp.int32(0), jnp.int32(0)
            for q in range(4):
                j = z * 32 + it * 4 + q
                key = jnp.broadcast_to(keys_ref[pl.ds(c * LANES + j, 1), :], (8, LANES))
                low, high = ends_ref[2 * c, j], ends_ref[2 * c + 1, j]
                lows.append(low)
                tiles.append(low >> 3)
                most = jnp.maximum(most, high - low + 1)
                many = jnp.maximum(many, (high >> 3) - (low >> 3) + 1)
                lanes_of.append((key >> 13) & 127)
                rows_of.append((key >> 20) - low)
                subrows.append((key >> 20) - (low >> 3) * 8 - sub)
                weights.append(jnp.where((key & 1) != 0, -scale, scale))

            def add_rows(first, count, eighth, eighths, acc, end=None):
                acc = list(acc)
                for q in range(4):
                    for u in range(count):
                        row = lows[q] + first + u
                        row = row if end is None else jnp.minimum(row, end)
                        hit = rows_of[q] == first + u
                        for t in range(2):
                            tile = tab[pl.ds(pl.multiple_of(row * 16 + 8 * t, 8), 8), :]
                            acc[q * 3 + t] = jnp.where(hit, lane_take(tile, lanes_of[q]), acc[q * 3 + t])
                    for u in range(eighths):
                        row = tiles[q] + eighth + u
                        row = row if end is None else jnp.minimum(row, end // 8)
                        tile = last[pl.ds(pl.multiple_of(row * 8, 8), 8), :]
                        hit = subrows[q] == (eighth + u) * 8
                        acc[q * 3 + 2] = jnp.where(hit, lane_take(tile, lanes_of[q]), acc[q * 3 + 2])
                return tuple(acc)

            acc = add_rows(0, PEEL, 0, EIGHTHS, (jnp.zeros((8, LANES), jnp.float32),) * 12)
            more = (jnp.maximum(most - PEEL, 0) + STEP - 1) // STEP
            more = jnp.maximum(more, many - EIGHTHS)

            def further(n, acc):
                return add_rows(PEEL + n * STEP, STEP, EIGHTHS + n, 1, acc, ROWS - 1)

            acc = lax.fori_loop(0, more, further, acc)
            base = it * (4 * COLS)
            for q in range(4):
                for t in range(2):
                    out[pl.ds(base + q + 32 * t, 8, stride=4), :] = acc[q * 3 + t] * weights[q]
                line = jnp.sum(acc[q * 3 + 2], axis=0, keepdims=True)
                out[pl.ds(base + q + 64, 1), :] = line * weights[q][0:1]
            return 0

        lax.fori_loop(0, 8, group, 0)


def slots_call(scale, off, cores, pos, ends, tab, last, keys):
    part = jax.ShapeDtypeStruct((8 * 4 * COLS, LANES), jnp.float32)
    return pl.pallas_call(
        lambda *refs: slots_kernel(scale, off, cores, *refs),
        out_shape=(part,) * len(cores),
        in_specs=[SMEM, SMEM, VMEM, VMEM, VMEM],
        out_specs=(VMEM,) * len(cores),
        compiler_params=pltpu.CompilerParams(vmem_limit_bytes=12 * 2**20),
        cost_estimate=COST,
        name=f"take_slots_{off}" + "".join(map(str, cores)),
    )(pos, ends, tab, last, keys)


def order_lines(rel, pos_ref, rank_ref, table, out, boxes):
    y, z = pos_ref[2], pos_ref[4]
    rows = 8 * COLS
    at = lax.broadcasted_iota(jnp.int32, (rows, LANES), 0)
    code = jnp.where(at >= rows // 2, 4, 0) + (at & 3)
    for i in range(8):
        line = z * 32 + ((y + rel) & 3) * 8 + i
        slot = jnp.broadcast_to(rank_ref[pl.ds(line, 1), :], (8, LANES))
        index = slot & 127
        pair = slot >> 10
        acc = [jnp.zeros((8, LANES), jnp.float32)] * COLS
        for n in range(4):
            hit = pair == n
            for t in range(COLS):
                tile = table[n * rows + 8 * t : n * rows + 8 * t + 8, :]
                acc[t] = jnp.where(hit, lane_take(tile, index), acc[t])
        boxes[i] = jnp.where(code == ((slot >> 7) & 7)[0:1], jnp.concatenate(acc, axis=0), 0.0)
        starts = [half * (rows // 2) + q for half in range(2) for q in range(4)]
        values = sum(boxes[i, pl.ds(first, 16, stride=4), :] for first in starts)
        for t in range(2):
            out[pl.ds(i + 64 * t, 8, stride=8), :] = values[8 * t : 8 * t + 8]
        out[128 + i : 129 + i, :] = sum(boxes[i, first + 64 : first + 65, :] for first in starts)


def order_first_kernel(rels, pos_ref, rank_ref, p0, p1, p2, p3, table, *refs):
    table[...] = (p0[...] + p1[...]) + (p2[...] + p3[...])
    for rel, out in zip(rels, refs):
        order_lines(rel, pos_ref, rank_ref, table, out, refs[-1])


def order_call(rel, pos, rank, *given):
    rows = 8 * COLS
    out = jax.ShapeDtypeStruct((rows, LANES), jnp.float32)
    table = jax.ShapeDtypeStruct((4 * rows, LANES), jnp.float32)
    first = len(given) > 1
    kernel = order_first_kernel if first else order_lines
    return pl.pallas_call(
        lambda *refs: kernel(rel, *refs),
        out_shape=(table,) + (out,) * len(rel) if first else out,
        in_specs=[SMEM] + [VMEM] * (1 + len(given)),
        out_specs=(VMEM,) * (1 + len(rel)) if first else VMEM,
        scratch_shapes=[pltpu.VMEM((8, rows, LANES), jnp.float32)],
        compiler_params=pltpu.CompilerParams(vmem_limit_bytes=8 * 2**20),
        cost_estimate=COST,
        name="given_order_far" if first else "given_order_own",
    )(pos, rank, *given)


def finish_kernel(factor, pos_ref, owners_ref, p0, p1, p2, p3, sketch, gram, table):
    core, y, x, z = pos_ref[1], pos_ref[2], pos_ref[3], pos_ref[4]
    table[0 : 8 * COLS, :] = (p0[...] + p1[...]) + (p2[...] + p3[...])
    table[8 * COLS :, :] = jnp.zeros((24 * 8 - 8 * COLS, LANES), jnp.float32)
    for h in range(2):
        sketch[:, h * LANES : (h + 1) * LANES] = table[pl.ds(2 * x + h, 24, stride=8), :][:COLS]
    pieces, lefts = ([], []), ([], [])
    for tx in range(4):
        for h in range(2):
            v = table[pl.ds(2 * tx + h, 24, stride=8), :]
            owner = owners_ref[y * 4 + tx, core, pl.ds(2 * z + h, 1), :]
            for n, term in enumerate(split(v)):
                wide = term.astype(jnp.float32)
                left = [jnp.where(owner == g, wide[:16], 0.0) for g in range(GROUPS)]
                lefts[n].append(jnp.concatenate(left, axis=0).astype(jnp.bfloat16))
                pieces[n].append(term)
    value = [jnp.concatenate(p, axis=1) for p in pieces]
    left = [jnp.concatenate(p, axis=1) for p in lefts]
    total = sum(
        lax.dot_general(value[p], left[q], (((1,), (1,)), ((), ())), preferred_element_type=jnp.float32)
        for p, q in ((0, 0), (0, 1), (1, 0))
    )
    total = factor * total
    for to in range(4):
        own = [total[8 * n : 8 * n + 8, 32 * to : 32 * to + 32] for n in range(3)]
        message = jnp.concatenate(own + [jnp.zeros((8, 32), jnp.float32)], axis=1)
        gram[to] = message


def finish_call(factor, pos, owners, parts):
    return pl.pallas_call(
        lambda *refs: finish_kernel(factor, *refs),
        out_shape=(
            jax.ShapeDtypeStruct((COLS, SIDE), jnp.float32),
            jax.ShapeDtypeStruct((4, 8, LANES), jnp.float32),
        ),
        in_specs=[SMEM] + [VMEM] * 5,
        out_specs=(VMEM,) * 2,
        scratch_shapes=[pltpu.VMEM((24 * 8, LANES), jnp.float32)],
        compiler_params=pltpu.CompilerParams(vmem_limit_bytes=8 * 2**20),
        name="rows_and_gram",
    )(pos, owners, *parts)


def gram_kernel(messages, out):
    total = jnp.sum(messages[...], axis=0)
    total = jnp.concatenate([total[:, 32 * n : 32 * n + 32] for n in range(3)], axis=0).T
    for g in range(2):
        out[g] = total[16 * g : 16 * g + 16, :COLS]


def gram_call(messages):
    return pl.pallas_call(
        gram_kernel,
        out_shape=jax.ShapeDtypeStruct((2, 16, COLS), jnp.float32),
        in_specs=[VMEM],
        out_specs=VMEM,
        compiler_params=pltpu.CompilerParams(vmem_limit_bytes=4 * 2**20),
        name="own_gram",
    )(messages)


def send(v, axis, off):
    return lax.ppermute(v, AXES, shift(axis, off))


def planes():
    return [[number(y, x, c, z) for y in range(4) for z in range(4)] for x in range(4) for c in range(2)]


def shards(basis, target, sign_bits, samples, owners):
    rows = basis.shape[1]
    total_samples = samples.shape[0]
    scale = 1.0 / math.sqrt(rows * 128)
    wide = lax.axis_index("wide")
    z = lax.axis_index("quad")
    core, x, y = wide & 1, (wide >> 1) & 3, wide >> 3
    pos = jnp.stack([wide * 4 + z, core, y, x, z, z, z, z]).astype(jnp.int32)

    tiles = basis.reshape(2, 8, 512, LANES).transpose(0, 2, 1, 3).reshape(8192, LANES)
    far = [samples.reshape(16, 2, 8, LANES), tiles, target.reshape(512, LANES), sign_bits.reshape(512, LANES)]
    far = [pltpu.with_memory_space_constraint(v, pltpu.HBM) for v in far]
    keys, ends, rank, tab, last = prepare_call(pos, *far)
    def after(v, *others):
        return lax.optimization_barrier((v,) + others)[0]

    def take(off, *cores):
        return slots_call(scale, off, cores, pos, ends, tab, last, keys)

    keep2, give2 = take(2, 0, 1)
    got2 = send(give2, "c", 1)
    give1, = take(1, 1)
    got1 = send(give1, "c", 1)
    both2 = keep2 + got2
    keys = after(keys, give1, both2)
    keep1, = take(1, 0)
    both1 = keep1 + got1
    keys = after(keys, both1)
    give3, = take(3, 1)
    got3 = send(give3, "c", 1)
    part2 = send(both2, "z", 2)
    keys = after(keys, give3, part2)
    keep3, = take(3, 0)
    both3 = keep3 + got3
    part1 = send(both1, "z", 1)
    part3 = send(both3, "z", 3)
    keys = after(keys, both3)
    keep, give = take(0, 0, 1)
    both0 = keep + send(give, "c", 1)
    rank = after(rank, keep, part1, part3)
    parts = [part2, part1, part3, both0]
    rels = (2, 1, 3)
    table, *lines = order_call(rels, pos, rank, *parts)
    got = [send(line, "y", rel) for line, rel in zip(lines, rels)]
    line = (order_call(0, pos, rank, table) + got[0]) + (got[1] + got[2])
    around = [line] + [send(line, "x", off) for off in (2, 1, 3)]
    sketch, gram = finish_call(GROUPS / total_samples, pos, owners.reshape(16, 2, 8, LANES), around)
    gram = jnp.concatenate([gram + send(gram, "c", 1)] * 4, axis=0)
    gram = lax.all_to_all(gram, AXES, 0, 0, tiled=True, axis_index_groups=planes())
    return sketch.T, gram_call(gram)


def solution(mesh):
    placed = (P(None, AXES), P(AXES), P(AXES), P(), P())
    return jax.shard_map(
        shards,
        mesh=mesh,
        in_specs=placed,
        out_specs=(P(AXES, None), P("quad", None, None)),
        check_vma=False,
    )
```

```python
import math

import jax
import jax.numpy as jnp
from jax import lax
from jax.experimental import pallas as pl
from jax.experimental.pallas import tpu as pltpu
from jax.sharding import PartitionSpec as P

GROUPS = 8
AXES = ("wide", "quad")
LANES = 128
COLS = 17
SIDE = 256
FETCHED = 36
PEEL = 20
STEP = 4
EIGHTHS = 4
ROWS = 512
ROWS_PAD = 536


def number(y, x, c, z):
    return ((y * 4 + x) * 2 + c) * 4 + z


def shift(axis, off):
    pairs = []
    for y in range(4):
        for x in range(4):
            for c in range(2):
                for z in range(4):
                    at = {"y": y, "x": x, "c": c, "z": z}
                    size = 2 if axis == "c" else 4
                    to = dict(at)
                    to[axis] = (at[axis] + (-off if c else off)) % size
                    pairs.append((number(**at), number(**to)))
    return pairs


def away(core, off):
    return jnp.where(core == 0, off, -off)


def fold(v):
    v = v ^ (v >> 8)
    v = v ^ (v >> 4)
    v = v ^ (v >> 2)
    v = v ^ (v >> 1)
    return v & 1


def lane_take(tile, index):
    return jnp.take_along_axis(tile, index, axis=1)


def bitonic_steps(v, sub, lane):
    for k in range(1, 13):
        for b in (k - 1, k):
            if b == 0 or b == 12:
                continue
            if b < 4:
                v[:] = [~t if (i >> b) & 1 else t for i, t in enumerate(v)]
            else:
                bit = (sub >> (b - 4)) if b < 7 else (lane >> (b - 7))
                m = -(bit & 1)
                v[:] = [t ^ m for t in v]
        for j in range(k - 1, -1, -1):
            if j < 4:
                new = list(v)
                for i in range(16):
                    if not (i >> j) & 1:
                        a, b = v[i], v[i | (1 << j)]
                        new[i] = jnp.minimum(a, b)
                        new[i | (1 << j)] = jnp.maximum(a, b)
                v[:] = new
            elif j < 7:
                d = 1 << (j - 4)
                up = (sub & d) != 0
                new = []
                for t in v:
                    prev = pltpu.roll(t, d, 0)
                    nxt = prev if d == 4 else pltpu.roll(t, 8 - d, 0)
                    new.append(jnp.where(up, jnp.maximum(t, prev), jnp.minimum(t, nxt)))
                v[:] = new
            else:
                d = 1 << (j - 7)
                up = (lane & d) != 0
                other = lane ^ d
                new = []
                for t in v:
                    o = lane_take(t, other)
                    new.append(jnp.where(up, jnp.maximum(t, o), jnp.minimum(t, o)))
                v[:] = new
            yield


def bitonic(v, sub, lane):
    for _ in bitonic_steps(v, sub, lane):
        pass
    return v


def swap_bits(t, sub, lane, p, q):
    sb, lb = (sub >> p) & 1, (lane >> q) & 1
    o = lane_take(t, lane ^ (1 << q))
    o = jnp.where(sb == 1, pltpu.roll(o, 1 << p, 0), pltpu.roll(o, 8 - (1 << p), 0))
    return jnp.where(sb == lb, t, o)


def split(x):
    hi = x.astype(jnp.bfloat16)
    lo = (x - hi.astype(jnp.float32)).astype(jnp.bfloat16)
    return hi, lo


def dot(a, b):
    return lax.dot_general(a, b, (((1,), (0,)), ((), ())), preferred_element_type=jnp.float32)


def prepare_kernel(
    pos_ref, samples_hbm, basis_hbm, target_hbm, bits_hbm, keys_ref, ends_ref, rank_ref, tab, last,
    samples_ref, basis_ref, target_ref, bits_ref, scratch, walsh_ref, flip_ref, sems,
):
    copies = [
        pltpu.make_async_copy(src, dst, sems.at[n])
        for n, (src, dst) in enumerate(
            ((samples_hbm, samples_ref), (bits_hbm, bits_ref), (target_hbm, target_ref), (basis_hbm, basis_ref))
        )
    ]
    for copy in copies:
        copy.start()

    me, core = pos_ref[0], pos_ref[1]
    sub = lax.broadcasted_iota(jnp.int32, (8, LANES), 0)
    lane = lax.broadcasted_iota(jnp.int32, (8, LANES), 1)
    def load(c):
        v = []
        for i in range(16):
            s = samples_ref[i, c]
            s = swap_bits(swap_bits(s, sub, lane, 1, 5), sub, lane, 2, 6)
            p = s & 65535
            place = (((p >> 7) & 1) << 15) | ((p >> 8) << 7) | (p & 127)
            odd = fold((s >> 16) & me)
            r = i * 256 + (sub & 1) * 128 + (sub >> 1) * 32 + (lane & 31)
            v.append((place << 13) | (r << 1) | odd)
        return v

    def store(c, v):
        for i in range(16):
            scratch[c, pl.ds(i, 8, stride=16), :] = v[i]
        ends_ref[2 * c : 2 * c + 1, :] = scratch[c, 0:1, :] >> 20
        ends_ref[2 * c + 1 : 2 * c + 2, :] = scratch[c, 127:128, :] >> 20
        keys_ref[c * LANES : (c + 1) * LANES, :] = scratch[c].T

    def flips_of(bh):
        return (1 - 2 * bits_ref[pl.ds(bh, SIDE, stride=2), :]).astype(jnp.float32)

    def mix(k):
        if k < 16:
            base = (k // 8) * 4096 + k % 8
            halves = [basis_ref[pl.ds(base + 8 * bh, SIDE, stride=16), :] for bh in range(2)]
        else:
            halves = [target_ref[pl.ds(bh, SIDE, stride=2), :] for bh in range(2)]
        x = jnp.concatenate(halves, axis=1) * flip_ref[...]
        hi, lo = split(x)
        walsh = walsh_ref[...]
        y = dot(hi, walsh) + dot(lo, walsh)
        hi, lo = split(y)
        z = dot(walsh, hi) + dot(walsh, lo)
        for bh in range(2):
            half = z[:, bh * LANES : (bh + 1) * LANES]
            if k < 16:
                tab[pl.ds(bh * SIDE * 16 + k, SIDE, stride=16), :] = half
            else:
                last[bh * SIDE : (bh + 1) * SIDE, :] = half

    a = lax.broadcasted_iota(jnp.int32, (SIDE, SIDE), 0)
    b = lax.broadcasted_iota(jnp.int32, (SIDE, SIDE), 1)
    walsh_ref[...] = (1 - 2 * fold(a & b)).astype(jnp.float32).astype(jnp.bfloat16)
    copies[0].wait()
    v, w = load(0), load(1)
    todo = list(range(COLS))
    for n, _ in enumerate(zip(bitonic_steps(v, sub, lane), bitonic_steps(w, sub, lane))):
        if n == FETCHED:
            for copy in copies[1:]:
                copy.wait()
            flip_ref[...] = jnp.concatenate([flips_of(0), flips_of(1)], axis=1)
        if n >= FETCHED and (n - FETCHED) % 5 == 0 and len(todo) > 9:
            mix(todo.pop(0))
    store(0, v)
    store(1, w)
    v = []
    for i in range(16):
        key = scratch[core, pl.ds(i, 8, stride=16), :]
        slot = (lane & 31) * LANES + sub * 16 + i
        v.append((((key >> 1) & 4095) << 12) | slot)
    for n, _ in enumerate(bitonic_steps(v, sub, lane)):
        if n % 9 == 0 and todo:
            mix(todo.pop(0))
    while todo:
        mix(todo.pop(0))
    for i in range(16):
        scratch[2, pl.ds(i, 8, stride=16), :] = v[i] & 4095
    rank_ref[...] = scratch[2].T
    tab[ROWS * 16 :, :] = jnp.zeros(((ROWS_PAD - ROWS) * 16, LANES), jnp.float32)
    last[ROWS:, :] = jnp.zeros((ROWS_PAD - ROWS, LANES), jnp.float32)


VMEM = pl.BlockSpec(memory_space=pltpu.VMEM)
SMEM = pl.BlockSpec(memory_space=pltpu.SMEM)
FAR = pl.BlockSpec(memory_space=pltpu.HBM)
COST = pl.CostEstimate(flops=1_000_000, bytes_accessed=1_000_000, transcendentals=0)


def prepare_call(pos, samples, basis, target, bits):
    return pl.pallas_call(
        prepare_kernel,
        out_shape=(
            jax.ShapeDtypeStruct((256, LANES), jnp.int32),
            jax.ShapeDtypeStruct((4, LANES), jnp.int32),
            jax.ShapeDtypeStruct((LANES, LANES), jnp.int32),
            jax.ShapeDtypeStruct((ROWS_PAD * 16, LANES), jnp.float32),
            jax.ShapeDtypeStruct((ROWS_PAD, LANES), jnp.float32),
        ),
        in_specs=[SMEM, FAR, FAR, FAR, FAR],
        out_specs=(VMEM,) * 5,
        scratch_shapes=[
            pltpu.VMEM((16, 2, 8, LANES), jnp.int32),
            pltpu.VMEM((8192, LANES), jnp.float32),
            pltpu.VMEM((512, LANES), jnp.float32),
            pltpu.VMEM((512, LANES), jnp.int32),
            pltpu.VMEM((3, LANES, LANES), jnp.int32),
            pltpu.VMEM((SIDE, SIDE), jnp.bfloat16),
            pltpu.VMEM((SIDE, SIDE), jnp.float32),
            pltpu.SemaphoreType.DMA((4,)),
        ],
        compiler_params=pltpu.CompilerParams(vmem_limit_bytes=24 * 2**20),
        cost_estimate=COST,
        name="sort_and_walsh",
    )(pos, samples, basis, target, bits)


def slots_kernel(scale, off, cores, pos_ref, ends_ref, tab, last, keys_ref, *outs):
    core = pos_ref[1]
    sub = lax.broadcasted_iota(jnp.int32, (8, LANES), 0)
    for rel_core, out in zip(cores, outs):
        c = core ^ rel_core
        z = (pos_ref[4] + away(c, off)) & 3

        def group(it, _, c=c, z=z, out=out):
            lows, tiles, lanes_of, rows_of, subrows, weights = [], [], [], [], [], []
            most, many = jnp.int32(0), jnp.int32(0)
            for q in range(4):
                j = z * 32 + it * 4 + q
                key = jnp.broadcast_to(keys_ref[pl.ds(c * LANES + j, 1), :], (8, LANES))
                low, high = ends_ref[2 * c, j], ends_ref[2 * c + 1, j]
                lows.append(low)
                tiles.append(low >> 3)
                most = jnp.maximum(most, high - low + 1)
                many = jnp.maximum(many, (high >> 3) - (low >> 3) + 1)
                lanes_of.append((key >> 13) & 127)
                rows_of.append((key >> 20) - low)
                subrows.append((key >> 20) - (low >> 3) * 8 - sub)
                weights.append(jnp.where((key & 1) != 0, -scale, scale))

            def add_rows(first, count, eighth, eighths, acc, end=None):
                acc = list(acc)
                for q in range(4):
                    for u in range(count):
                        row = lows[q] + first + u
                        row = row if end is None else jnp.minimum(row, end)
                        hit = rows_of[q] == first + u
                        for t in range(2):
                            tile = tab[pl.ds(pl.multiple_of(row * 16 + 8 * t, 8), 8), :]
                            acc[q * 3 + t] = jnp.where(hit, lane_take(tile, lanes_of[q]), acc[q * 3 + t])
                    for u in range(eighths):
                        row = tiles[q] + eighth + u
                        row = row if end is None else jnp.minimum(row, end // 8)
                        tile = last[pl.ds(pl.multiple_of(row * 8, 8), 8), :]
                        hit = subrows[q] == (eighth + u) * 8
                        acc[q * 3 + 2] = jnp.where(hit, lane_take(tile, lanes_of[q]), acc[q * 3 + 2])
                return tuple(acc)

            acc = add_rows(0, PEEL, 0, EIGHTHS, (jnp.zeros((8, LANES), jnp.float32),) * 12)
            more = (jnp.maximum(most - PEEL, 0) + STEP - 1) // STEP
            more = jnp.maximum(more, many - EIGHTHS)

            def further(n, acc):
                return add_rows(PEEL + n * STEP, STEP, EIGHTHS + n, 1, acc, ROWS - 1)

            acc = lax.fori_loop(0, more, further, acc)
            base = it * (4 * COLS)
            for q in range(4):
                for t in range(2):
                    out[pl.ds(base + q + 32 * t, 8, stride=4), :] = acc[q * 3 + t] * weights[q]
                line = jnp.sum(acc[q * 3 + 2], axis=0, keepdims=True)
                out[pl.ds(base + q + 64, 1), :] = line * weights[q][0:1]
            return 0

        lax.fori_loop(0, 8, group, 0)


def slots_call(scale, off, cores, pos, ends, tab, last, keys):
    part = jax.ShapeDtypeStruct((8 * 4 * COLS, LANES), jnp.float32)
    return pl.pallas_call(
        lambda *refs: slots_kernel(scale, off, cores, *refs),
        out_shape=(part,) * len(cores),
        in_specs=[SMEM, SMEM, VMEM, VMEM, VMEM],
        out_specs=(VMEM,) * len(cores),
        compiler_params=pltpu.CompilerParams(vmem_limit_bytes=12 * 2**20),
        cost_estimate=COST,
        name=f"take_slots_{off}" + "".join(map(str, cores)),
    )(pos, ends, tab, last, keys)


def order_lines(rel, pos_ref, rank_ref, table, out, boxes):
    y, z = pos_ref[2] + away(pos_ref[1], rel), pos_ref[4]
    rows = 8 * COLS
    at = lax.broadcasted_iota(jnp.int32, (rows, LANES), 0)
    code = jnp.where(at >= rows // 2, 4, 0) + (at & 3)
    for i in range(8):
        line = z * 32 + (y & 3) * 8 + i
        slot = jnp.broadcast_to(rank_ref[pl.ds(line, 1), :], (8, LANES))
        index = slot & 127
        pair = slot >> 10
        acc = [jnp.zeros((8, LANES), jnp.float32)] * COLS
        for n in range(4):
            hit = pair == n
            for t in range(COLS):
                tile = table[n * rows + 8 * t : n * rows + 8 * t + 8, :]
                acc[t] = jnp.where(hit, lane_take(tile, index), acc[t])
        boxes[i] = jnp.where(code == ((slot >> 7) & 7)[0:1], jnp.concatenate(acc, axis=0), 0.0)
        starts = [half * (rows // 2) + q for half in range(2) for q in range(4)]
        values = sum(boxes[i, pl.ds(first, 16, stride=4), :] for first in starts)
        for t in range(2):
            out[pl.ds(i + 64 * t, 8, stride=8), :] = values[8 * t : 8 * t + 8]
        out[128 + i : 129 + i, :] = sum(boxes[i, first + 64 : first + 65, :] for first in starts)


def order_first_kernel(rels, pos_ref, rank_ref, p0, p1, p2, p3, table, *refs):
    table[...] = (p0[...] + p1[...]) + (p2[...] + p3[...])
    for rel, out in zip(rels, refs):
        order_lines(rel, pos_ref, rank_ref, table, out, refs[-1])


def order_call(rel, pos, rank, *given):
    rows = 8 * COLS
    out = jax.ShapeDtypeStruct((rows, LANES), jnp.float32)
    table = jax.ShapeDtypeStruct((4 * rows, LANES), jnp.float32)
    first = len(given) > 1
    kernel = order_first_kernel if first else order_lines
    return pl.pallas_call(
        lambda *refs: kernel(rel, *refs),
        out_shape=(table,) + (out,) * len(rel) if first else out,
        in_specs=[SMEM] + [VMEM] * (1 + len(given)),
        out_specs=(VMEM,) * (1 + len(rel)) if first else VMEM,
        scratch_shapes=[pltpu.VMEM((8, rows, LANES), jnp.float32)],
        compiler_params=pltpu.CompilerParams(vmem_limit_bytes=8 * 2**20),
        cost_estimate=COST,
        name="given_order_far" if first else "given_order_own",
    )(pos, rank, *given)


def finish_kernel(factor, pos_ref, owners_ref, p0, p1, p2, p3, sketch, gram, table):
    core, y, x, z = pos_ref[1], pos_ref[2], pos_ref[3], pos_ref[4]
    table[0 : 8 * COLS, :] = (p0[...] + p1[...]) + (p2[...] + p3[...])
    table[8 * COLS :, :] = jnp.zeros((24 * 8 - 8 * COLS, LANES), jnp.float32)
    for h in range(2):
        sketch[:, h * LANES : (h + 1) * LANES] = table[pl.ds(2 * x + h, 24, stride=8), :][:COLS]
    pieces, lefts = ([], []), ([], [])
    for tx in range(4):
        for h in range(2):
            v = table[pl.ds(2 * tx + h, 24, stride=8), :]
            owner = owners_ref[y * 4 + tx, core, pl.ds(2 * z + h, 1), :]
            for n, term in enumerate(split(v)):
                wide = term.astype(jnp.float32)
                left = [jnp.where(owner == g, wide[:16], 0.0) for g in range(GROUPS)]
                lefts[n].append(jnp.concatenate(left, axis=0).astype(jnp.bfloat16))
                pieces[n].append(term)
    value = [jnp.concatenate(p, axis=1) for p in pieces]
    left = [jnp.concatenate(p, axis=1) for p in lefts]
    total = sum(
        lax.dot_general(value[p], left[q], (((1,), (1,)), ((), ())), preferred_element_type=jnp.float32)
        for p, q in ((0, 0), (0, 1), (1, 0))
    )
    total = factor * total
    for to in range(4):
        own = [total[8 * n : 8 * n + 8, 32 * to : 32 * to + 32] for n in range(3)]
        message = jnp.concatenate(own + [jnp.zeros((8, 32), jnp.float32)], axis=1)
        gram[to] = message


def finish_call(factor, pos, owners, parts):
    return pl.pallas_call(
        lambda *refs: finish_kernel(factor, *refs),
        out_shape=(
            jax.ShapeDtypeStruct((COLS, SIDE), jnp.float32),
            jax.ShapeDtypeStruct((4, 8, LANES), jnp.float32),
        ),
        in_specs=[SMEM] + [VMEM] * 5,
        out_specs=(VMEM,) * 2,
        scratch_shapes=[pltpu.VMEM((24 * 8, LANES), jnp.float32)],
        compiler_params=pltpu.CompilerParams(vmem_limit_bytes=8 * 2**20),
        name="rows_and_gram",
    )(pos, owners, *parts)


def gram_kernel(messages, out):
    total = jnp.sum(messages[...], axis=0)
    total = jnp.concatenate([total[:, 32 * n : 32 * n + 32] for n in range(3)], axis=0).T
    for g in range(2):
        out[g] = total[16 * g : 16 * g + 16, :COLS]


def gram_call(messages):
    return pl.pallas_call(
        gram_kernel,
        out_shape=jax.ShapeDtypeStruct((2, 16, COLS), jnp.float32),
        in_specs=[VMEM],
        out_specs=VMEM,
        compiler_params=pltpu.CompilerParams(vmem_limit_bytes=4 * 2**20),
        name="own_gram",
    )(messages)


def send(v, axis, off):
    return lax.ppermute(v, AXES, shift(axis, off))


def planes():
    return [[number(y, x, c, z) for y in range(4) for z in range(4)] for x in range(4) for c in range(2)]


def shards(basis, target, sign_bits, samples, owners):
    rows = basis.shape[1]
    total_samples = samples.shape[0]
    scale = 1.0 / math.sqrt(rows * 128)
    wide = lax.axis_index("wide")
    z = lax.axis_index("quad")
    core, x, y = wide & 1, (wide >> 1) & 3, wide >> 3
    pos = jnp.stack([wide * 4 + z, core, y, x, z, z, z, z]).astype(jnp.int32)

    tiles = basis.reshape(2, 8, 512, LANES).transpose(0, 2, 1, 3).reshape(8192, LANES)
    far = [samples.reshape(16, 2, 8, LANES), tiles, target.reshape(512, LANES), sign_bits.reshape(512, LANES)]
    far = [pltpu.with_memory_space_constraint(v, pltpu.HBM) for v in far]
    keys, ends, rank, tab, last = prepare_call(pos, *far)
    def after(v, *others):
        return lax.optimization_barrier((v,) + others)[0]

    def take(off, *cores):
        return slots_call(scale, off, cores, pos, ends, tab, last, keys)

    keep2, give2 = take(2, 0, 1)
    got2 = send(give2, "c", 1)
    give1, = take(1, 1)
    got1 = send(give1, "c", 1)
    both2 = keep2 + got2
    keys = after(keys, give1, both2)
    keep1, = take(1, 0)
    both1 = keep1 + got1
    keys = after(keys, both1)
    give3, = take(3, 1)
    got3 = send(give3, "c", 1)
    part2 = send(both2, "z", 2)
    keys = after(keys, give3, part2)
    keep3, = take(3, 0)
    both3 = keep3 + got3
    part1 = send(both1, "z", 1)
    part3 = send(both3, "z", 3)
    keys = after(keys, both3)
    keep, give = take(0, 0, 1)
    both0 = keep + send(give, "c", 1)
    rank = after(rank, keep, part1, part3)
    parts = [part2, part1, part3, both0]
    rels = (2, 1, 3)
    table, *lines = order_call(rels, pos, rank, *parts)
    got = [send(line, "y", rel) for line, rel in zip(lines, rels)]
    line = (order_call(0, pos, rank, table) + got[0]) + (got[1] + got[2])
    around = [line] + [send(line, "x", off) for off in (2, 1, 3)]
    sketch, gram = finish_call(GROUPS / total_samples, pos, owners.reshape(16, 2, 8, LANES), around)
    gram = jnp.concatenate([gram + send(gram, "c", 1)] * 4, axis=0)
    gram = lax.all_to_all(gram, AXES, 0, 0, tiled=True, axis_index_groups=planes())
    return sketch.T, gram_call(gram)


def solution(mesh):
    placed = (P(None, AXES), P(AXES), P(AXES), P(), P())
    return jax.shard_map(
        shards,
        mesh=mesh,
        in_specs=placed,
        out_specs=(P(AXES, None), P("quad", None, None)),
        check_vma=False,
    )
```

```python
import math

import jax
import jax.numpy as jnp
from jax import lax
from jax.experimental import pallas as pl
from jax.experimental.pallas import tpu as pltpu
from jax.sharding import PartitionSpec as P

GROUPS = 8
AXES = ("wide", "quad")
LANES = 128
COLS = 17
SIDE = 256
FETCHED = 36
PEEL = 20
OTHER = (0, 2, 3, 1)
STEP = 4
EIGHTHS = 4
ROWS = 512
ROWS_PAD = 536


def number(y, x, c, z):
    return ((y * 4 + x) * 2 + c) * 4 + z


def shift(axis, off):
    pairs = []
    for y in range(4):
        for x in range(4):
            for c in range(2):
                for z in range(4):
                    at = {"y": y, "x": x, "c": c, "z": z}
                    size = 2 if axis == "c" else 4
                    to = dict(at)
                    to[axis] = (at[axis] + (OTHER[off] if c and axis != "c" else off)) % size
                    pairs.append((number(**at), number(**to)))
    return pairs


def away(core, off):
    return jnp.where(core == 0, off, OTHER[off])


def fold(v):
    v = v ^ (v >> 8)
    v = v ^ (v >> 4)
    v = v ^ (v >> 2)
    v = v ^ (v >> 1)
    return v & 1


def lane_take(tile, index):
    return jnp.take_along_axis(tile, index, axis=1)


def bitonic_steps(v, sub, lane):
    for k in range(1, 13):
        for b in (k - 1, k):
            if b == 0 or b == 12:
                continue
            if b < 4:
                v[:] = [~t if (i >> b) & 1 else t for i, t in enumerate(v)]
            else:
                bit = (sub >> (b - 4)) if b < 7 else (lane >> (b - 7))
                m = -(bit & 1)
                v[:] = [t ^ m for t in v]
        for j in range(k - 1, -1, -1):
            if j < 4:
                new = list(v)
                for i in range(16):
                    if not (i >> j) & 1:
                        a, b = v[i], v[i | (1 << j)]
                        new[i] = jnp.minimum(a, b)
                        new[i | (1 << j)] = jnp.maximum(a, b)
                v[:] = new
            elif j < 7:
                d = 1 << (j - 4)
                up = (sub & d) != 0
                new = []
                for t in v:
                    prev = pltpu.roll(t, d, 0)
                    nxt = prev if d == 4 else pltpu.roll(t, 8 - d, 0)
                    new.append(jnp.where(up, jnp.maximum(t, prev), jnp.minimum(t, nxt)))
                v[:] = new
            else:
                d = 1 << (j - 7)
                up = (lane & d) != 0
                other = lane ^ d
                new = []
                for t in v:
                    o = lane_take(t, other)
                    new.append(jnp.where(up, jnp.maximum(t, o), jnp.minimum(t, o)))
                v[:] = new
            yield


def bitonic(v, sub, lane):
    for _ in bitonic_steps(v, sub, lane):
        pass
    return v


def swap_bits(t, sub, lane, p, q):
    sb, lb = (sub >> p) & 1, (lane >> q) & 1
    o = lane_take(t, lane ^ (1 << q))
    o = jnp.where(sb == 1, pltpu.roll(o, 1 << p, 0), pltpu.roll(o, 8 - (1 << p), 0))
    return jnp.where(sb == lb, t, o)


def split(x):
    hi = x.astype(jnp.bfloat16)
    lo = (x - hi.astype(jnp.float32)).astype(jnp.bfloat16)
    return hi, lo


def dot(a, b):
    return lax.dot_general(a, b, (((1,), (0,)), ((), ())), preferred_element_type=jnp.float32)


def prepare_kernel(
    pos_ref, samples_hbm, basis_hbm, target_hbm, bits_hbm, keys_ref, ends_ref, rank_ref, tab, last,
    samples_ref, basis_ref, target_ref, bits_ref, scratch, walsh_ref, flip_ref, sems,
):
    copies = [
        pltpu.make_async_copy(src, dst, sems.at[n])
        for n, (src, dst) in enumerate(
            ((samples_hbm, samples_ref), (bits_hbm, bits_ref), (target_hbm, target_ref), (basis_hbm, basis_ref))
        )
    ]
    for copy in copies:
        copy.start()

    me, core = pos_ref[0], pos_ref[1]
    sub = lax.broadcasted_iota(jnp.int32, (8, LANES), 0)
    lane = lax.broadcasted_iota(jnp.int32, (8, LANES), 1)
    def load(c):
        v = []
        for i in range(16):
            s = samples_ref[i, c]
            s = swap_bits(swap_bits(s, sub, lane, 1, 5), sub, lane, 2, 6)
            p = s & 65535
            place = (((p >> 7) & 1) << 15) | ((p >> 8) << 7) | (p & 127)
            odd = fold((s >> 16) & me)
            r = i * 256 + (sub & 1) * 128 + (sub >> 1) * 32 + (lane & 31)
            v.append((place << 13) | (r << 1) | odd)
        return v

    def store(c, v):
        for i in range(16):
            scratch[c, pl.ds(i, 8, stride=16), :] = v[i]
        ends_ref[2 * c : 2 * c + 1, :] = scratch[c, 0:1, :] >> 20
        ends_ref[2 * c + 1 : 2 * c + 2, :] = scratch[c, 127:128, :] >> 20
        keys_ref[c * LANES : (c + 1) * LANES, :] = scratch[c].T

    def flips_of(bh):
        return (1 - 2 * bits_ref[pl.ds(bh, SIDE, stride=2), :]).astype(jnp.float32)

    def mix(k):
        if k < 16:
            base = (k // 8) * 4096 + k % 8
            halves = [basis_ref[pl.ds(base + 8 * bh, SIDE, stride=16), :] for bh in range(2)]
        else:
            halves = [target_ref[pl.ds(bh, SIDE, stride=2), :] for bh in range(2)]
        x = jnp.concatenate(halves, axis=1) * flip_ref[...]
        hi, lo = split(x)
        walsh = walsh_ref[...]
        y = dot(hi, walsh) + dot(lo, walsh)
        hi, lo = split(y)
        z = dot(walsh, hi) + dot(walsh, lo)
        for bh in range(2):
            half = z[:, bh * LANES : (bh + 1) * LANES]
            if k < 16:
                tab[pl.ds(bh * SIDE * 16 + k, SIDE, stride=16), :] = half
            else:
                last[bh * SIDE : (bh + 1) * SIDE, :] = half

    a = lax.broadcasted_iota(jnp.int32, (SIDE, SIDE), 0)
    b = lax.broadcasted_iota(jnp.int32, (SIDE, SIDE), 1)
    walsh_ref[...] = (1 - 2 * fold(a & b)).astype(jnp.float32).astype(jnp.bfloat16)
    copies[0].wait()
    v, w = load(0), load(1)
    todo = list(range(COLS))
    for n, _ in enumerate(zip(bitonic_steps(v, sub, lane), bitonic_steps(w, sub, lane))):
        if n == FETCHED:
            for copy in copies[1:]:
                copy.wait()
            flip_ref[...] = jnp.concatenate([flips_of(0), flips_of(1)], axis=1)
        if n >= FETCHED and (n - FETCHED) % 5 == 0 and len(todo) > 9:
            mix(todo.pop(0))
    store(0, v)
    store(1, w)
    v = []
    for i in range(16):
        key = scratch[core, pl.ds(i, 8, stride=16), :]
        slot = (lane & 31) * LANES + sub * 16 + i
        v.append((((key >> 1) & 4095) << 12) | slot)
    for n, _ in enumerate(bitonic_steps(v, sub, lane)):
        if n % 9 == 0 and todo:
            mix(todo.pop(0))
    while todo:
        mix(todo.pop(0))
    for i in range(16):
        scratch[2, pl.ds(i, 8, stride=16), :] = v[i] & 4095
    rank_ref[...] = scratch[2].T
    tab[ROWS * 16 :, :] = jnp.zeros(((ROWS_PAD - ROWS) * 16, LANES), jnp.float32)
    last[ROWS:, :] = jnp.zeros((ROWS_PAD - ROWS, LANES), jnp.float32)


VMEM = pl.BlockSpec(memory_space=pltpu.VMEM)
SMEM = pl.BlockSpec(memory_space=pltpu.SMEM)
FAR = pl.BlockSpec(memory_space=pltpu.HBM)
COST = pl.CostEstimate(flops=1_000_000, bytes_accessed=1_000_000, transcendentals=0)


def prepare_call(pos, samples, basis, target, bits):
    return pl.pallas_call(
        prepare_kernel,
        out_shape=(
            jax.ShapeDtypeStruct((256, LANES), jnp.int32),
            jax.ShapeDtypeStruct((4, LANES), jnp.int32),
            jax.ShapeDtypeStruct((LANES, LANES), jnp.int32),
            jax.ShapeDtypeStruct((ROWS_PAD * 16, LANES), jnp.float32),
            jax.ShapeDtypeStruct((ROWS_PAD, LANES), jnp.float32),
        ),
        in_specs=[SMEM, FAR, FAR, FAR, FAR],
        out_specs=(VMEM,) * 5,
        scratch_shapes=[
            pltpu.VMEM((16, 2, 8, LANES), jnp.int32),
            pltpu.VMEM((8192, LANES), jnp.float32),
            pltpu.VMEM((512, LANES), jnp.float32),
            pltpu.VMEM((512, LANES), jnp.int32),
            pltpu.VMEM((3, LANES, LANES), jnp.int32),
            pltpu.VMEM((SIDE, SIDE), jnp.bfloat16),
            pltpu.VMEM((SIDE, SIDE), jnp.float32),
            pltpu.SemaphoreType.DMA((4,)),
        ],
        compiler_params=pltpu.CompilerParams(vmem_limit_bytes=24 * 2**20),
        cost_estimate=COST,
        name="sort_and_walsh",
    )(pos, samples, basis, target, bits)


def slots_kernel(scale, off, cores, pos_ref, ends_ref, tab, last, keys_ref, *outs):
    core = pos_ref[1]
    sub = lax.broadcasted_iota(jnp.int32, (8, LANES), 0)
    for rel_core, out in zip(cores, outs):
        c = core ^ rel_core
        z = (pos_ref[4] + away(c, off)) & 3

        def group(it, _, c=c, z=z, out=out):
            lows, tiles, lanes_of, rows_of, subrows, weights = [], [], [], [], [], []
            most, many = jnp.int32(0), jnp.int32(0)
            for q in range(4):
                j = z * 32 + it * 4 + q
                key = jnp.broadcast_to(keys_ref[pl.ds(c * LANES + j, 1), :], (8, LANES))
                low, high = ends_ref[2 * c, j], ends_ref[2 * c + 1, j]
                lows.append(low)
                tiles.append(low >> 3)
                most = jnp.maximum(most, high - low + 1)
                many = jnp.maximum(many, (high >> 3) - (low >> 3) + 1)
                lanes_of.append((key >> 13) & 127)
                rows_of.append((key >> 20) - low)
                subrows.append((key >> 20) - (low >> 3) * 8 - sub)
                weights.append(jnp.where((key & 1) != 0, -scale, scale))

            def add_rows(first, count, eighth, eighths, acc, end=None):
                acc = list(acc)
                for q in range(4):
                    for u in range(count):
                        row = lows[q] + first + u
                        row = row if end is None else jnp.minimum(row, end)
                        hit = rows_of[q] == first + u
                        for t in range(2):
                            tile = tab[pl.ds(pl.multiple_of(row * 16 + 8 * t, 8), 8), :]
                            acc[q * 3 + t] = jnp.where(hit, lane_take(tile, lanes_of[q]), acc[q * 3 + t])
                    for u in range(eighths):
                        row = tiles[q] + eighth + u
                        row = row if end is None else jnp.minimum(row, end // 8)
                        tile = last[pl.ds(pl.multiple_of(row * 8, 8), 8), :]
                        hit = subrows[q] == (eighth + u) * 8
                        acc[q * 3 + 2] = jnp.where(hit, lane_take(tile, lanes_of[q]), acc[q * 3 + 2])
                return tuple(acc)

            acc = add_rows(0, PEEL, 0, EIGHTHS, (jnp.zeros((8, LANES), jnp.float32),) * 12)
            more = (jnp.maximum(most - PEEL, 0) + STEP - 1) // STEP
            more = jnp.maximum(more, many - EIGHTHS)

            def further(n, acc):
                return add_rows(PEEL + n * STEP, STEP, EIGHTHS + n, 1, acc, ROWS - 1)

            acc = lax.fori_loop(0, more, further, acc)
            base = it * (4 * COLS)
            for q in range(4):
                for t in range(2):
                    out[pl.ds(base + q + 32 * t, 8, stride=4), :] = acc[q * 3 + t] * weights[q]
                line = jnp.sum(acc[q * 3 + 2], axis=0, keepdims=True)
                out[pl.ds(base + q + 64, 1), :] = line * weights[q][0:1]
            return 0

        lax.fori_loop(0, 8, group, 0)


def slots_call(scale, off, cores, pos, ends, tab, last, keys):
    part = jax.ShapeDtypeStruct((8 * 4 * COLS, LANES), jnp.float32)
    return pl.pallas_call(
        lambda *refs: slots_kernel(scale, off, cores, *refs),
        out_shape=(part,) * len(cores),
        in_specs=[SMEM, SMEM, VMEM, VMEM, VMEM],
        out_specs=(VMEM,) * len(cores),
        compiler_params=pltpu.CompilerParams(vmem_limit_bytes=12 * 2**20),
        cost_estimate=COST,
        name=f"take_slots_{off}" + "".join(map(str, cores)),
    )(pos, ends, tab, last, keys)


def order_lines(rel, pos_ref, rank_ref, table, out, boxes):
    y, z = pos_ref[2] + away(pos_ref[1], rel), pos_ref[4]
    rows = 8 * COLS
    at = lax.broadcasted_iota(jnp.int32, (rows, LANES), 0)
    code = jnp.where(at >= rows // 2, 4, 0) + (at & 3)
    for i in range(8):
        line = z * 32 + (y & 3) * 8 + i
        slot = jnp.broadcast_to(rank_ref[pl.ds(line, 1), :], (8, LANES))
        index = slot & 127
        pair = slot >> 10
        acc = [jnp.zeros((8, LANES), jnp.float32)] * COLS
        for n in range(4):
            hit = pair == n
            for t in range(COLS):
                tile = table[n * rows + 8 * t : n * rows + 8 * t + 8, :]
                acc[t] = jnp.where(hit, lane_take(tile, index), acc[t])
        boxes[i] = jnp.where(code == ((slot >> 7) & 7)[0:1], jnp.concatenate(acc, axis=0), 0.0)
        starts = [half * (rows // 2) + q for half in range(2) for q in range(4)]
        values = sum(boxes[i, pl.ds(first, 16, stride=4), :] for first in starts)
        for t in range(2):
            out[pl.ds(i + 64 * t, 8, stride=8), :] = values[8 * t : 8 * t + 8]
        out[128 + i : 129 + i, :] = sum(boxes[i, first + 64 : first + 65, :] for first in starts)


def order_first_kernel(rels, pos_ref, rank_ref, p0, p1, p2, p3, table, *refs):
    table[...] = (p0[...] + p1[...]) + (p2[...] + p3[...])
    for rel, out in zip(rels, refs):
        order_lines(rel, pos_ref, rank_ref, table, out, refs[-1])


def order_call(rel, pos, rank, *given):
    rows = 8 * COLS
    out = jax.ShapeDtypeStruct((rows, LANES), jnp.float32)
    table = jax.ShapeDtypeStruct((4 * rows, LANES), jnp.float32)
    first = len(given) > 1
    kernel = order_first_kernel if first else order_lines
    return pl.pallas_call(
        lambda *refs: kernel(rel, *refs),
        out_shape=(table,) + (out,) * len(rel) if first else out,
        in_specs=[SMEM] + [VMEM] * (1 + len(given)),
        out_specs=(VMEM,) * (1 + len(rel)) if first else VMEM,
        scratch_shapes=[pltpu.VMEM((8, rows, LANES), jnp.float32)],
        compiler_params=pltpu.CompilerParams(vmem_limit_bytes=8 * 2**20),
        cost_estimate=COST,
        name="given_order_far" if first else "given_order_own",
    )(pos, rank, *given)


def finish_kernel(factor, pos_ref, owners_ref, p0, p1, p2, p3, sketch, gram, table):
    core, y, x, z = pos_ref[1], pos_ref[2], pos_ref[3], pos_ref[4]
    table[0 : 8 * COLS, :] = (p0[...] + p1[...]) + (p2[...] + p3[...])
    table[8 * COLS :, :] = jnp.zeros((24 * 8 - 8 * COLS, LANES), jnp.float32)
    for h in range(2):
        sketch[:, h * LANES : (h + 1) * LANES] = table[pl.ds(2 * x + h, 24, stride=8), :][:COLS]
    pieces, lefts = ([], []), ([], [])
    for tx in range(4):
        for h in range(2):
            v = table[pl.ds(2 * tx + h, 24, stride=8), :]
            owner = owners_ref[y * 4 + tx, core, pl.ds(2 * z + h, 1), :]
            for n, term in enumerate(split(v)):
                wide = term.astype(jnp.float32)
                left = [jnp.where(owner == g, wide[:16], 0.0) for g in range(GROUPS)]
                lefts[n].append(jnp.concatenate(left, axis=0).astype(jnp.bfloat16))
                pieces[n].append(term)
    value = [jnp.concatenate(p, axis=1) for p in pieces]
    left = [jnp.concatenate(p, axis=1) for p in lefts]
    total = sum(
        lax.dot_general(value[p], left[q], (((1,), (1,)), ((), ())), preferred_element_type=jnp.float32)
        for p, q in ((0, 0), (0, 1), (1, 0))
    )
    total = factor * total
    for to in range(4):
        own = [total[8 * n : 8 * n + 8, 32 * to : 32 * to + 32] for n in range(3)]
        message = jnp.concatenate(own + [jnp.zeros((8, 32), jnp.float32)], axis=1)
        gram[to] = message


def finish_call(factor, pos, owners, parts):
    return pl.pallas_call(
        lambda *refs: finish_kernel(factor, *refs),
        out_shape=(
            jax.ShapeDtypeStruct((COLS, SIDE), jnp.float32),
            jax.ShapeDtypeStruct((4, 8, LANES), jnp.float32),
        ),
        in_specs=[SMEM] + [VMEM] * 5,
        out_specs=(VMEM,) * 2,
        scratch_shapes=[pltpu.VMEM((24 * 8, LANES), jnp.float32)],
        compiler_params=pltpu.CompilerParams(vmem_limit_bytes=8 * 2**20),
        name="rows_and_gram",
    )(pos, owners, *parts)


def gram_kernel(messages, out):
    total = jnp.sum(messages[...], axis=0)
    total = jnp.concatenate([total[:, 32 * n : 32 * n + 32] for n in range(3)], axis=0).T
    for g in range(2):
        out[g] = total[16 * g : 16 * g + 16, :COLS]


def gram_call(messages):
    return pl.pallas_call(
        gram_kernel,
        out_shape=jax.ShapeDtypeStruct((2, 16, COLS), jnp.float32),
        in_specs=[VMEM],
        out_specs=VMEM,
        compiler_params=pltpu.CompilerParams(vmem_limit_bytes=4 * 2**20),
        name="own_gram",
    )(messages)


def send(v, axis, off):
    return lax.ppermute(v, AXES, shift(axis, off))


def planes():
    return [[number(y, x, c, z) for y in range(4) for z in range(4)] for x in range(4) for c in range(2)]


def shards(basis, target, sign_bits, samples, owners):
    rows = basis.shape[1]
    total_samples = samples.shape[0]
    scale = 1.0 / math.sqrt(rows * 128)
    wide = lax.axis_index("wide")
    z = lax.axis_index("quad")
    core, x, y = wide & 1, (wide >> 1) & 3, wide >> 3
    pos = jnp.stack([wide * 4 + z, core, y, x, z, z, z, z]).astype(jnp.int32)

    tiles = basis.reshape(2, 8, 512, LANES).transpose(0, 2, 1, 3).reshape(8192, LANES)
    far = [samples.reshape(16, 2, 8, LANES), tiles, target.reshape(512, LANES), sign_bits.reshape(512, LANES)]
    far = [pltpu.with_memory_space_constraint(v, pltpu.HBM) for v in far]
    keys, ends, rank, tab, last = prepare_call(pos, *far)
    def after(v, *others):
        return lax.optimization_barrier((v,) + others)[0]

    def take(off, *cores):
        return slots_call(scale, off, cores, pos, ends, tab, last, keys)

    keep2, give2 = take(2, 0, 1)
    got2 = send(give2, "c", 1)
    give1, = take(1, 1)
    got1 = send(give1, "c", 1)
    both2 = keep2 + got2
    keys = after(keys, give1, both2)
    keep1, = take(1, 0)
    both1 = keep1 + got1
    keys = after(keys, both1)
    give3, = take(3, 1)
    got3 = send(give3, "c", 1)
    part2 = send(both2, "z", 2)
    keys = after(keys, give3, part2)
    keep3, = take(3, 0)
    both3 = keep3 + got3
    part1 = send(both1, "z", 1)
    part3 = send(both3, "z", 3)
    keys = after(keys, both3)
    keep, give = take(0, 0, 1)
    both0 = keep + send(give, "c", 1)
    rank = after(rank, keep, part1, part3)
    parts = [part2, part1, part3, both0]
    rels = (2, 1, 3)
    table, *lines = order_call(rels, pos, rank, *parts)
    got = [send(line, "y", rel) for line, rel in zip(lines, rels)]
    line = (order_call(0, pos, rank, table) + got[0]) + (got[1] + got[2])
    around = [line] + [send(line, "x", off) for off in (2, 1, 3)]
    sketch, gram = finish_call(GROUPS / total_samples, pos, owners.reshape(16, 2, 8, LANES), around)
    gram = jnp.concatenate([gram + send(gram, "c", 1)] * 4, axis=0)
    gram = lax.all_to_all(gram, AXES, 0, 0, tiled=True, axis_index_groups=planes())
    return sketch.T, gram_call(gram)


def solution(mesh):
    placed = (P(None, AXES), P(AXES), P(AXES), P(), P())
    return jax.shard_map(
        shards,
        mesh=mesh,
        in_specs=placed,
        out_specs=(P(AXES, None), P("quad", None, None)),
        check_vma=False,
    )
```

```python
import math

import jax
import jax.numpy as jnp
from jax import lax
from jax.experimental import pallas as pl
from jax.experimental.pallas import tpu as pltpu
from jax.sharding import PartitionSpec as P

GROUPS = 8
AXES = ("wide", "quad")
LANES = 128
COLS = 17
SIDE = 256
FETCHED = 36
PEEL = 20
OTHER = (0, 2, 3, 1)
STEP = 4
EIGHTHS = 4
ROWS = 512
ROWS_PAD = 536


def number(y, x, c, z):
    return ((y * 4 + x) * 2 + c) * 4 + z


def shift(axis, off):
    pairs = []
    for y in range(4):
        for x in range(4):
            for c in range(2):
                for z in range(4):
                    at = {"y": y, "x": x, "c": c, "z": z}
                    size = 2 if axis == "c" else 4
                    to = dict(at)
                    to[axis] = (at[axis] + (OTHER[off] if c and axis != "c" else off)) % size
                    pairs.append((number(**at), number(**to)))
    return pairs


def away(core, off):
    return jnp.where(core == 0, off, OTHER[off])


def fold(v):
    v = v ^ (v >> 8)
    v = v ^ (v >> 4)
    v = v ^ (v >> 2)
    v = v ^ (v >> 1)
    return v & 1


def lane_take(tile, index):
    return jnp.take_along_axis(tile, index, axis=1)


def bitonic_steps(v, sub, lane):
    for k in range(1, 13):
        for b in (k - 1, k):
            if b == 0 or b == 12:
                continue
            if b < 4:
                v[:] = [~t if (i >> b) & 1 else t for i, t in enumerate(v)]
            else:
                bit = (sub >> (b - 4)) if b < 7 else (lane >> (b - 7))
                m = -(bit & 1)
                v[:] = [t ^ m for t in v]
        for j in range(k - 1, -1, -1):
            if j < 4:
                new = list(v)
                for i in range(16):
                    if not (i >> j) & 1:
                        a, b = v[i], v[i | (1 << j)]
                        new[i] = jnp.minimum(a, b)
                        new[i | (1 << j)] = jnp.maximum(a, b)
                v[:] = new
            elif j < 7:
                d = 1 << (j - 4)
                up = (sub & d) != 0
                new = []
                for t in v:
                    prev = pltpu.roll(t, d, 0)
                    nxt = prev if d == 4 else pltpu.roll(t, 8 - d, 0)
                    new.append(jnp.where(up, jnp.maximum(t, prev), jnp.minimum(t, nxt)))
                v[:] = new
            else:
                d = 1 << (j - 7)
                up = (lane & d) != 0
                other = lane ^ d
                new = []
                for t in v:
                    o = lane_take(t, other)
                    new.append(jnp.where(up, jnp.maximum(t, o), jnp.minimum(t, o)))
                v[:] = new
            yield


def bitonic(v, sub, lane):
    for _ in bitonic_steps(v, sub, lane):
        pass
    return v


def swap_bits(t, sub, lane, p, q):
    sb, lb = (sub >> p) & 1, (lane >> q) & 1
    o = lane_take(t, lane ^ (1 << q))
    o = jnp.where(sb == 1, pltpu.roll(o, 1 << p, 0), pltpu.roll(o, 8 - (1 << p), 0))
    return jnp.where(sb == lb, t, o)


def split(x):
    hi = x.astype(jnp.bfloat16)
    lo = (x - hi.astype(jnp.float32)).astype(jnp.bfloat16)
    return hi, lo


def dot(a, b):
    return lax.dot_general(a, b, (((1,), (0,)), ((), ())), preferred_element_type=jnp.float32)


def prepare_kernel(
    pos_ref, samples_hbm, basis_hbm, target_hbm, bits_hbm, keys_ref, ends_ref, rank_ref, tab, last,
    samples_ref, basis_ref, target_ref, bits_ref, scratch, walsh_ref, flip_ref, sems,
):
    copies = [
        pltpu.make_async_copy(src, dst, sems.at[n])
        for n, (src, dst) in enumerate(
            ((samples_hbm, samples_ref), (bits_hbm, bits_ref), (target_hbm, target_ref), (basis_hbm, basis_ref))
        )
    ]
    for copy in copies:
        copy.start()

    me, core = pos_ref[0], pos_ref[1]
    sub = lax.broadcasted_iota(jnp.int32, (8, LANES), 0)
    lane = lax.broadcasted_iota(jnp.int32, (8, LANES), 1)
    def load(c):
        v = []
        for i in range(16):
            s = samples_ref[i, c]
            s = swap_bits(swap_bits(s, sub, lane, 1, 5), sub, lane, 2, 6)
            p = s & 65535
            place = (((p >> 7) & 1) << 15) | ((p >> 8) << 7) | (p & 127)
            odd = fold((s >> 16) & me)
            r = i * 256 + (sub & 1) * 128 + (sub >> 1) * 32 + (lane & 31)
            v.append((place << 13) | (r << 1) | odd)
        return v

    def store(c, v):
        for i in range(16):
            scratch[c, pl.ds(i, 8, stride=16), :] = v[i]
        ends_ref[2 * c : 2 * c + 1, :] = scratch[c, 0:1, :] >> 20
        ends_ref[2 * c + 1 : 2 * c + 2, :] = scratch[c, 127:128, :] >> 20
        keys_ref[c * LANES : (c + 1) * LANES, :] = scratch[c].T

    def flips_of(bh):
        return (1 - 2 * bits_ref[pl.ds(bh, SIDE, stride=2), :]).astype(jnp.float32)

    def mix(k):
        if k < 16:
            base = (k // 8) * 4096 + k % 8
            halves = [basis_ref[pl.ds(base + 8 * bh, SIDE, stride=16), :] for bh in range(2)]
        else:
            halves = [target_ref[pl.ds(bh, SIDE, stride=2), :] for bh in range(2)]
        x = jnp.concatenate(halves, axis=1) * flip_ref[...]
        hi, lo = split(x)
        walsh = walsh_ref[...]
        y = dot(hi, walsh) + dot(lo, walsh)
        hi, lo = split(y)
        z = dot(walsh, hi) + dot(walsh, lo)
        for bh in range(2):
            half = z[:, bh * LANES : (bh + 1) * LANES]
            if k < 16:
                tab[pl.ds(bh * SIDE * 16 + k, SIDE, stride=16), :] = half
            else:
                last[bh * SIDE : (bh + 1) * SIDE, :] = half

    a = lax.broadcasted_iota(jnp.int32, (SIDE, SIDE), 0)
    b = lax.broadcasted_iota(jnp.int32, (SIDE, SIDE), 1)
    walsh_ref[...] = (1 - 2 * fold(a & b)).astype(jnp.float32).astype(jnp.bfloat16)
    copies[0].wait()
    v, w = load(0), load(1)
    todo = list(range(COLS))
    for n, _ in enumerate(zip(bitonic_steps(v, sub, lane), bitonic_steps(w, sub, lane))):
        if n == FETCHED:
            for copy in copies[1:]:
                copy.wait()
            flip_ref[...] = jnp.concatenate([flips_of(0), flips_of(1)], axis=1)
        if n >= FETCHED and (n - FETCHED) % 5 == 0 and len(todo) > 9:
            mix(todo.pop(0))
    store(0, v)
    store(1, w)
    v = []
    for i in range(16):
        key = scratch[core, pl.ds(i, 8, stride=16), :]
        slot = (lane & 31) * LANES + sub * 16 + i
        v.append((((key >> 1) & 4095) << 12) | slot)
    for n, _ in enumerate(bitonic_steps(v, sub, lane)):
        if n % 9 == 0 and todo:
            mix(todo.pop(0))
    while todo:
        mix(todo.pop(0))
    for i in range(16):
        scratch[2, pl.ds(i, 8, stride=16), :] = v[i] & 4095
    rank_ref[...] = scratch[2].T
    tab[ROWS * 16 :, :] = jnp.zeros(((ROWS_PAD - ROWS) * 16, LANES), jnp.float32)
    last[ROWS:, :] = jnp.zeros((ROWS_PAD - ROWS, LANES), jnp.float32)


VMEM = pl.BlockSpec(memory_space=pltpu.VMEM)
SMEM = pl.BlockSpec(memory_space=pltpu.SMEM)
FAR = pl.BlockSpec(memory_space=pltpu.HBM)
COST = pl.CostEstimate(flops=1_000_000, bytes_accessed=1_000_000, transcendentals=0)


def prepare_call(pos, samples, basis, target, bits):
    return pl.pallas_call(
        prepare_kernel,
        out_shape=(
            jax.ShapeDtypeStruct((256, LANES), jnp.int32),
            jax.ShapeDtypeStruct((4, LANES), jnp.int32),
            jax.ShapeDtypeStruct((LANES, LANES), jnp.int32),
            jax.ShapeDtypeStruct((ROWS_PAD * 16, LANES), jnp.float32),
            jax.ShapeDtypeStruct((ROWS_PAD, LANES), jnp.float32),
        ),
        in_specs=[SMEM, FAR, FAR, FAR, FAR],
        out_specs=(VMEM,) * 5,
        scratch_shapes=[
            pltpu.VMEM((16, 2, 8, LANES), jnp.int32),
            pltpu.VMEM((8192, LANES), jnp.float32),
            pltpu.VMEM((512, LANES), jnp.float32),
            pltpu.VMEM((512, LANES), jnp.int32),
            pltpu.VMEM((3, LANES, LANES), jnp.int32),
            pltpu.VMEM((SIDE, SIDE), jnp.bfloat16),
            pltpu.VMEM((SIDE, SIDE), jnp.float32),
            pltpu.SemaphoreType.DMA((4,)),
        ],
        compiler_params=pltpu.CompilerParams(vmem_limit_bytes=24 * 2**20),
        cost_estimate=COST,
        name="sort_and_walsh",
    )(pos, samples, basis, target, bits)


def slots_kernel(scale, off, cores, pos_ref, ends_ref, tab, last, keys_ref, *outs):
    core = pos_ref[1]
    sub = lax.broadcasted_iota(jnp.int32, (8, LANES), 0)
    for rel_core, out in zip(cores, outs):
        c = core ^ rel_core
        z = (pos_ref[4] + away(c, off)) & 3

        def group(it, _, c=c, z=z, out=out):
            lows, tiles, lanes_of, rows_of, subrows, weights = [], [], [], [], [], []
            most, many = jnp.int32(0), jnp.int32(0)
            for q in range(4):
                j = z * 32 + it * 4 + q
                key = jnp.broadcast_to(keys_ref[pl.ds(c * LANES + j, 1), :], (8, LANES))
                low, high = ends_ref[2 * c, j], ends_ref[2 * c + 1, j]
                lows.append(low)
                tiles.append(low >> 3)
                most = jnp.maximum(most, high - low + 1)
                many = jnp.maximum(many, (high >> 3) - (low >> 3) + 1)
                lanes_of.append((key >> 13) & 127)
                rows_of.append((key >> 20) - low)
                subrows.append((key >> 20) - (low >> 3) * 8 - sub)
                weights.append(jnp.where((key & 1) != 0, -scale, scale))

            def add_rows(first, count, eighth, eighths, acc, end=None):
                acc = list(acc)
                for q in range(4):
                    for u in range(count):
                        row = lows[q] + first + u
                        row = row if end is None else jnp.minimum(row, end)
                        hit = rows_of[q] == first + u
                        for t in range(2):
                            tile = tab[pl.ds(pl.multiple_of(row * 16 + 8 * t, 8), 8), :]
                            acc[q * 3 + t] = jnp.where(hit, lane_take(tile, lanes_of[q]), acc[q * 3 + t])
                    for u in range(eighths):
                        row = tiles[q] + eighth + u
                        row = row if end is None else jnp.minimum(row, end // 8)
                        tile = last[pl.ds(pl.multiple_of(row * 8, 8), 8), :]
                        hit = subrows[q] == (eighth + u) * 8
                        acc[q * 3 + 2] = jnp.where(hit, lane_take(tile, lanes_of[q]), acc[q * 3 + 2])
                return tuple(acc)

            acc = add_rows(0, PEEL, 0, EIGHTHS, (jnp.zeros((8, LANES), jnp.float32),) * 12)
            more = (jnp.maximum(most - PEEL, 0) + STEP - 1) // STEP
            more = jnp.maximum(more, many - EIGHTHS)

            def further(n, acc):
                return add_rows(PEEL + n * STEP, STEP, EIGHTHS + n, 1, acc, ROWS - 1)

            acc = lax.fori_loop(0, more, further, acc)
            base = it * (4 * COLS)
            for q in range(4):
                for t in range(2):
                    out[pl.ds(base + q + 32 * t, 8, stride=4), :] = acc[q * 3 + t] * weights[q]
                line = jnp.sum(acc[q * 3 + 2], axis=0, keepdims=True)
                out[pl.ds(base + q + 64, 1), :] = line * weights[q][0:1]
            return 0

        lax.fori_loop(0, 8, group, 0)


def slots_call(scale, off, cores, pos, ends, tab, last, keys):
    part = jax.ShapeDtypeStruct((8 * 4 * COLS, LANES), jnp.float32)
    return pl.pallas_call(
        lambda *refs: slots_kernel(scale, off, cores, *refs),
        out_shape=(part,) * len(cores),
        in_specs=[SMEM, SMEM, VMEM, VMEM, VMEM],
        out_specs=(VMEM,) * len(cores),
        compiler_params=pltpu.CompilerParams(vmem_limit_bytes=12 * 2**20),
        cost_estimate=COST,
        name=f"take_slots_{off}" + "".join(map(str, cores)),
    )(pos, ends, tab, last, keys)


def order_lines(rel, pos_ref, rank_ref, table, out, boxes):
    y, z = pos_ref[2] + away(pos_ref[1], rel), pos_ref[4]
    rows = 8 * COLS
    at = lax.broadcasted_iota(jnp.int32, (rows, LANES), 0)
    code = jnp.where(at >= rows // 2, 4, 0) + (at & 3)
    for i in range(8):
        line = z * 32 + (y & 3) * 8 + i
        slot = jnp.broadcast_to(rank_ref[pl.ds(line, 1), :], (8, LANES))
        index = slot & 127
        pair = slot >> 10
        acc = [jnp.zeros((8, LANES), jnp.float32)] * COLS
        for n in range(4):
            hit = pair == n
            for t in range(COLS):
                tile = table[n * rows + 8 * t : n * rows + 8 * t + 8, :]
                acc[t] = jnp.where(hit, lane_take(tile, index), acc[t])
        boxes[i] = jnp.where(code == ((slot >> 7) & 7)[0:1], jnp.concatenate(acc, axis=0), 0.0)
        starts = [half * (rows // 2) + q for half in range(2) for q in range(4)]
        values = sum(boxes[i, pl.ds(first, 16, stride=4), :] for first in starts)
        for t in range(2):
            out[pl.ds(i + 64 * t, 8, stride=8), :] = values[8 * t : 8 * t + 8]
        out[128 + i : 129 + i, :] = sum(boxes[i, first + 64 : first + 65, :] for first in starts)


def order_first_kernel(rels, pos_ref, rank_ref, p0, p1, p2, p3, table, *refs):
    table[...] = (p0[...] + p1[...]) + (p2[...] + p3[...])
    for rel, out in zip(rels, refs):
        order_lines(rel, pos_ref, rank_ref, table, out, refs[-1])


def order_call(rel, pos, rank, *given):
    rows = 8 * COLS
    out = jax.ShapeDtypeStruct((rows, LANES), jnp.float32)
    table = jax.ShapeDtypeStruct((4 * rows, LANES), jnp.float32)
    first = len(given) > 1
    kernel = order_first_kernel if first else order_lines
    return pl.pallas_call(
        lambda *refs: kernel(rel, *refs),
        out_shape=(table,) + (out,) * len(rel) if first else out,
        in_specs=[SMEM] + [VMEM] * (1 + len(given)),
        out_specs=(VMEM,) * (1 + len(rel)) if first else VMEM,
        scratch_shapes=[pltpu.VMEM((8, rows, LANES), jnp.float32)],
        compiler_params=pltpu.CompilerParams(vmem_limit_bytes=8 * 2**20),
        cost_estimate=COST,
        name="given_order_far" if first else "given_order_own",
    )(pos, rank, *given)


def finish_kernel(factor, pos_ref, owners_ref, p0, p1, p2, p3, sketch, gram, table):
    core, y, x, z = pos_ref[1], pos_ref[2], pos_ref[3], pos_ref[4]
    table[0 : 8 * COLS, :] = (p0[...] + p1[...]) + (p2[...] + p3[...])
    table[8 * COLS :, :] = jnp.zeros((24 * 8 - 8 * COLS, LANES), jnp.float32)
    for h in range(2):
        sketch[:, h * LANES : (h + 1) * LANES] = table[pl.ds(2 * x + h, 24, stride=8), :][:COLS]
    pieces, lefts = ([], []), ([], [])
    for tx in range(4):
        for h in range(2):
            v = table[pl.ds(2 * tx + h, 24, stride=8), :]
            owner = owners_ref[y * 4 + tx, core, pl.ds(2 * z + h, 1), :]
            for n, term in enumerate(split(v)):
                wide = term.astype(jnp.float32)
                left = [jnp.where(owner == g, wide[:16], 0.0) for g in range(GROUPS)]
                lefts[n].append(jnp.concatenate(left, axis=0).astype(jnp.bfloat16))
                pieces[n].append(term)
    value = [jnp.concatenate(p, axis=1) for p in pieces]
    left = [jnp.concatenate(p, axis=1) for p in lefts]
    total = sum(
        lax.dot_general(value[p], left[q], (((1,), (1,)), ((), ())), preferred_element_type=jnp.float32)
        for p, q in ((0, 0), (0, 1), (1, 0))
    )
    total = factor * total
    for to in range(4):
        own = [total[8 * n : 8 * n + 8, 32 * to : 32 * to + 32] for n in range(3)]
        message = jnp.concatenate(own + [jnp.zeros((8, 32), jnp.float32)], axis=1)
        gram[to] = message


def finish_call(factor, pos, owners, parts):
    return pl.pallas_call(
        lambda *refs: finish_kernel(factor, *refs),
        out_shape=(
            jax.ShapeDtypeStruct((COLS, SIDE), jnp.float32),
            jax.ShapeDtypeStruct((4, 8, LANES), jnp.float32),
        ),
        in_specs=[SMEM] + [VMEM] * 5,
        out_specs=(VMEM,) * 2,
        scratch_shapes=[pltpu.VMEM((24 * 8, LANES), jnp.float32)],
        compiler_params=pltpu.CompilerParams(vmem_limit_bytes=8 * 2**20),
        name="rows_and_gram",
    )(pos, owners, *parts)


def gram_kernel(messages, out):
    total = jnp.sum(messages[...], axis=0)
    total = jnp.concatenate([total[:, 32 * n : 32 * n + 32] for n in range(3)], axis=0).T
    for g in range(2):
        out[g] = total[16 * g : 16 * g + 16, :COLS]


def gram_call(messages):
    return pl.pallas_call(
        gram_kernel,
        out_shape=jax.ShapeDtypeStruct((2, 16, COLS), jnp.float32),
        in_specs=[VMEM],
        out_specs=VMEM,
        compiler_params=pltpu.CompilerParams(vmem_limit_bytes=4 * 2**20),
        name="own_gram",
    )(messages)


def send(v, axis, off):
    return lax.ppermute(v, AXES, shift(axis, off))


def planes():
    return [[number(y, x, c, z) for y in range(4) for z in range(4)] for x in range(4) for c in range(2)]


def shards(basis, target, sign_bits, samples, owners):
    rows = basis.shape[1]
    total_samples = samples.shape[0]
    scale = 1.0 / math.sqrt(rows * 128)
    wide = lax.axis_index("wide")
    z = lax.axis_index("quad")
    core, x, y = wide & 1, (wide >> 1) & 3, wide >> 3
    pos = jnp.stack([wide * 4 + z, core, y, x, z, z, z, z]).astype(jnp.int32)

    tiles = basis.reshape(2, 8, 512, LANES).transpose(0, 2, 1, 3).reshape(8192, LANES)
    far = [samples.reshape(16, 2, 8, LANES), tiles, target.reshape(512, LANES), sign_bits.reshape(512, LANES)]
    far = [pltpu.with_memory_space_constraint(v, pltpu.HBM) for v in far]
    keys, ends, rank, tab, last = prepare_call(pos, *far)
    def after(v, *others):
        return lax.optimization_barrier((v,) + others)[0]

    def take(off, *cores):
        return slots_call(scale, off, cores, pos, ends, tab, last, keys)

    keep2, give2 = take(2, 0, 1)
    got2 = send(give2, "c", 1)
    give1, = take(1, 1)
    got1 = send(give1, "c", 1)
    both2 = keep2 + got2
    keys = after(keys, give1, both2)
    keep1, = take(1, 0)
    both1 = keep1 + got1
    keys = after(keys, both1)
    give3, = take(3, 1)
    got3 = send(give3, "c", 1)
    part2 = send(both2, "z", 2)
    keys = after(keys, give3, part2)
    keep3, = take(3, 0)
    both3 = keep3 + got3
    part1 = send(both1, "z", 1)
    part3 = send(both3, "z", 3)
    keys = after(keys, both3)
    give, = take(0, 1)
    got0 = send(give, "c", 1)
    keys = after(keys, give)
    keep, = take(0, 0)
    both0 = keep + got0
    rank = after(rank, keep, part1, part3)
    parts = [part2, part1, part3, both0]
    rels = (2, 1, 3)
    table, *lines = order_call(rels, pos, rank, *parts)
    got = [send(line, "y", rel) for line, rel in zip(lines, rels)]
    line = (order_call(0, pos, rank, table) + got[0]) + (got[1] + got[2])
    around = [line] + [send(line, "x", off) for off in (2, 1, 3)]
    sketch, gram = finish_call(GROUPS / total_samples, pos, owners.reshape(16, 2, 8, LANES), around)
    gram = jnp.concatenate([gram + send(gram, "c", 1)] * 4, axis=0)
    gram = lax.all_to_all(gram, AXES, 0, 0, tiled=True, axis_index_groups=planes())
    return sketch.T, gram_call(gram)


def solution(mesh):
    placed = (P(None, AXES), P(AXES), P(AXES), P(), P())
    return jax.shard_map(
        shards,
        mesh=mesh,
        in_specs=placed,
        out_specs=(P(AXES, None), P("quad", None, None)),
        check_vma=False,
    )
```
